256 devices in a mesh: layer: 2 (over z_lo), latent: 32 (over x, y, core), token: 4 (over z_hi).
Axes of the slice: x: 4, y: 4, z: 8 (z_hi: 4, z_lo: 2; z = z_hi * 2 + z_lo), core: 2. Of those that a mesh axis runs over, the one named last changes fastest.
Arguments:
- resid_in: bfloat16 [2, 1024, 2304], P('layer', 'token', 'latent'), may hold values from -300 to 300
- clt_gain: float32 [2, 2304], P('layer'), may hold values from 0.1 to 1.9
- enc_w: bfloat16 [2, 2304, 16384], P('layer', None, 'latent'), may hold values from -0.125 to 0.125
- enc_b: float32 [2, 16384], P('layer', 'latent'), may hold values from -3 to 3
- dec_same: bfloat16 [2, 16384, 2304], P('layer', 'latent'), may hold values from -0.09375 to 0.09375
- dec_next: bfloat16 [16384, 2304], P('latent'), may hold values from -0.09375 to 0.09375
- frozen_sum: bfloat16 [1024, 2304], P('token', 'latent'), may hold values from -300 to 300
- mlp_gain: float32 [2304], P('latent'), may hold values from 0.1 to 1.9
- w_gate: bfloat16 [2304, 9216], P(None, ('layer', 'latent')), may hold values from -0.125 to 0.125
- w_up: bfloat16 [2304, 9216], P(None, ('layer', 'latent')), may hold values from -0.125 to 0.125
- w_down: bfloat16 [9216, 2304], P(('layer', 'latent')), may hold values from -0.1875 to 0.1875
Outputs:
- latents: bfloat16 [2, 1024, 16384], P('layer', 'token', 'latent')
- recon: bfloat16 [2, 1024, 2304], P('layer', 'token', 'latent')
- mlp_out: bfloat16 [1024, 2304], P('token', ('layer', 'latent'))
The draws below stay inside these ranges and needn't reach their ends.
All inputs are finite; a program needn't handle non-finite values.
Results may differ from the reference program's by a relative error of at most 0.0074.
Values may be sent and summed in bfloat16 or wider, within the bound.
A program may use at most 64 MiB of HBM per device.

```python
import math
import jax
import jax.numpy as jnp
from jax import lax

D = 2304
HID = 9216
FEAT = 16384
LAYERS = 2
TOKENS = 1024


def scaled_field(key, row_count, col_count, salt, low, high):
    key = jax.random.fold_in(key, salt)
    key_rows, key_cols, key_base = jax.random.split(key, 3)
    row_scale = jnp.exp(jax.random.uniform(key_rows, (row_count, 1), jnp.float32, math.log(low), math.log(high)))
    ramp = jnp.exp(math.log(4.0) * jnp.arange(col_count, dtype=jnp.float32) / (col_count - 1))
    jitter = jnp.exp(jax.random.uniform(key_cols, (col_count,), jnp.float32, math.log(0.6), math.log(1.5)))
    base = jnp.clip(jax.random.normal(key_base, (row_count, col_count), jnp.float32), -4.0, 4.0)
    return base * row_scale * ramp * jitter


def draw_resid_in(key, part):
    field = scaled_field(key, LAYERS * TOKENS, D, 11, 0.5, 8.0)
    return field.reshape(LAYERS, TOKENS, D).astype(jnp.bfloat16)


def draw_frozen_sum(key, part):
    return scaled_field(key, TOKENS, D, 23, 0.3, 3.0).astype(jnp.bfloat16)


def spiked(array, own_key, source, target, shards_of, factor):
    def block_of(axis_at):
        return (jnp.arange(array.shape[axis_at]) // (array.shape[axis_at] // shards_of)).reshape((-1,) + (1,) * (array.ndim - 1 - axis_at))

    near = jax.random.permutation(own_key, shards_of)[block_of(target)]
    second = (block_of(target) + shards_of // 2) % shards_of
    return jnp.where((block_of(source) == near) | (block_of(source) == second), factor * array, array)


def block_levels(own_key, extent, cuts, least, top_value):
    gain = 1.0
    for position, shards_of in cuts:
        draws = jax.random.uniform(jax.random.fold_in(jax.random.fold_in(own_key, 6), position), (shards_of,), jnp.float32, least / len(cuts), top_value / len(cuts))
        gain = gain * jnp.repeat(jnp.exp(draws), extent[position] // shards_of).reshape((-1,) + (1,) * (len(extent) - 1 - position))
    return gain


def bell_draw(own_key, shape, spread, most, shards=(), kind=jnp.bfloat16):
    values = jax.random.normal(own_key, shape, jnp.float32) * spread
    if len(shards) > 0:
        values = block_levels(own_key, shape, shards, -0.22, 0.18) * values
    return jnp.clip(values, min=-most, max=most).astype(kind)


def heavy_noise(stream_key, dims, spread, limit, cuts, heavy, kind=jnp.bfloat16):
    drawn = spread * jax.random.normal(stream_key, dims, jnp.float32)
    if cuts:
        drawn = drawn * block_levels(stream_key, dims, cuts, -0.22, 0.18)
    return jnp.clip(spiked(drawn, jax.random.fold_in(stream_key, 3), *heavy), -limit, limit).astype(kind)


def setup_inputs(seed: int = 0) -> dict:
    arg_keys = jax.random.split(jax.random.key(seed), 12)
    resid_in = draw_resid_in(jax.random.fold_in(arg_keys[11], 71), 0)
    clt_gain = jnp.clip(1.0 + 0.18 * jax.random.normal(arg_keys[1], (LAYERS, D), jnp.float32), 0.1, 1.9)
    enc_w = bell_draw(arg_keys[2], (LAYERS, D, FEAT), D ** -0.5, 0.125, ((0, 2), (2, 32)))
    enc_b = bell_draw(arg_keys[3], (LAYERS, FEAT), 0.5, 3.0, ((0, 2), (1, 32)), jnp.float32)
    dec_same = heavy_noise(arg_keys[4], (LAYERS, FEAT, D), FEAT ** -0.5, 0.09375, ((0, 2), (1, 32)), (1, 2, 32, 2.75))
    dec_next = heavy_noise(arg_keys[5], (FEAT, D), FEAT ** -0.5, 0.09375, ((0, 32),), (0, 1, 32, 2.75))
    frozen_sum = draw_frozen_sum(jax.random.fold_in(arg_keys[11], 71), 0)
    mlp_gain = jnp.clip(1.0 + 0.18 * jax.random.normal(arg_keys[7], (D,), jnp.float32), 0.1, 1.9)
    w_gate = bell_draw(arg_keys[8], (D, HID), D ** -0.5, 0.125, ((1, 64),))
    w_up = bell_draw(arg_keys[9], (D, HID), D ** -0.5, 0.125, ((1, 64),))
    w_down = heavy_noise(arg_keys[10], (HID, D), HID ** -0.5, 0.1875, ((0, 64),), (0, 1, 64, 4.0))
    return {"resid_in": resid_in, "clt_gain": clt_gain, "enc_w": enc_w, "enc_b": enc_b, "dec_same": dec_same, "dec_next": dec_next, "frozen_sum": frozen_sum, "mlp_gain": mlp_gain, "w_gate": w_gate, "w_up": w_up, "w_down": w_down}


def inv_rms(values):
    return lax.rsqrt(lax.optimization_barrier(jnp.mean(values * values, axis=-1, keepdims=True)) + 1e-06)

def reference(resid_in, clt_gain, enc_w, enc_b, dec_same, dec_next, frozen_sum, mlp_gain, w_gate, w_up, w_down):
    layer_lats = []
    for source in range(LAYERS):
        values = resid_in[source].astype(jnp.float32)
        gated = (values * clt_gain[source]).astype(jnp.bfloat16)
        pre_act = inv_rms(values) * jnp.dot(gated, enc_w[source], preferred_element_type=jnp.float32) + enc_b[source]
        layer_lats.append(jnp.maximum(pre_act, 0.0).astype(jnp.bfloat16))
    recon_zero = jnp.dot(layer_lats[0], dec_same[0], preferred_element_type=jnp.float32)
    recon_one = jnp.dot(layer_lats[0], dec_next, preferred_element_type=jnp.float32) + jnp.dot(layer_lats[1], dec_same[1], preferred_element_type=jnp.float32)
    recon = jnp.stack([recon_zero, recon_one]).astype(jnp.bfloat16)
    mixed = frozen_sum.astype(jnp.float32) + recon_zero + recon_one
    normed = (mixed * mlp_gain).astype(jnp.bfloat16)
    scale_rows = inv_rms(mixed)
    gate_pre = scale_rows * jnp.dot(normed, w_gate, preferred_element_type=jnp.float32)
    up_pre = scale_rows * jnp.dot(normed, w_up, preferred_element_type=jnp.float32)
    hidden = (jax.nn.gelu(gate_pre, approximate=True) * up_pre).astype(jnp.bfloat16)
    mlp_out = jnp.dot(hidden, w_down, preferred_element_type=jnp.float32).astype(jnp.bfloat16)
    return (jnp.stack(layer_lats), recon, mlp_out)
```

```python
import jax
import jax.numpy as jnp
from jax import lax
from jax.experimental import pallas as pl
from jax.experimental.pallas import tpu as pltpu
from jax.sharding import PartitionSpec as P

D = 2304
TOK = 256
HALF = 128
CHIP = 144
OWN = 72
PAD = 80
LAT = 512
EPS = 1e-06
MESH = pl.DeviceIdType.MESH
F32 = jnp.float32
BF16 = jnp.bfloat16
TN = (((0,), (0,)), ((), ()))
NN = (((1,), (0,)), ((), ()))

SINGLES_A = [(1, 0), (3, 0), (2, 0)]
SINGLES_B = [(0, 1), (0, 3), (0, 2)]
DIAGONALS = [(1, 1), (3, 3), (1, 3), (3, 1), (1, 2), (2, 1), (3, 2), (2, 3), (2, 2)]
FAR_FIRST = [(a, b) for a in (2, 1, 3, 0) for b in (2, 1, 3, 0)]


def kernel(
    resid, gain, encb, frozen, mgain, enc, dec_s, dec_n, w_gate, w_up, w_down,
    lat_out, recon_out, mlp_out,
    resid_v, gain_v, encb_v, frozen_v, mgain_v, enc_v, dec_s_v, dec_n_v, wg_v, wu_v, wd_v,
    gain_b, encb_b, lb, g1, lat_v, lat_t,
    fz_send, fz_recv, mg_send, mg_recv,
    prod, ys, yr, keep, s1, r1, s2, r2,
    z_send, z_recv, rc_send, rc_recv, recon_v,
    sq_a, sq_b, sq_d, g2, fin_send, fin_recv, out_v,
    in_sem, ag_s, ag_r, d2_s, d2_r, rs_s, rs_d, rs_1, rs_2,
    ag2_s, ag2_r, ag2_d, sq_s, sq_r, ms_s, ms_r,
):
    layer = lax.axis_index("layer")
    q = lax.axis_index("latent")
    core = lax.rem(q, 2)
    chip = lax.div(q, 2)
    cy = lax.rem(chip, 4)
    cx = lax.div(chip, 4)
    first = core == 0

    def chip_at(a, b):
        dx = jnp.where(first, a, b)
        dy = jnp.where(first, b, a)
        return lax.rem(cx + dx, 4) * 4 + lax.rem(cy + dy, 4)

    def along_a(d):
        return {"latent": chip_at(d, 0) * 2 + core}

    def along_b(d):
        return {"latent": chip_at(0, d) * 2 + core}

    sibling = {"latent": chip * 2 + 1 - core}
    across = {"layer": 1 - layer}
    across_sib = {"layer": 1 - layer, "latent": chip * 2 + 1 - core}
    own_lanes = pl.ds(pl.multiple_of(core * HALF, HALF), HALF)
    sib_lanes = pl.ds(pl.multiple_of((1 - core) * HALF, HALF), HALF)

    sends = []

    def send(src, dst, ssem, rsem, dev):
        copy = pltpu.make_async_remote_copy(
            src_ref=src, dst_ref=dst, send_sem=ssem, recv_sem=rsem, device_id=dev, device_id_type=MESH
        )
        copy.start()
        return copy

    def arrived(dst, ssem, rsem):
        pltpu.make_async_remote_copy(
            src_ref=dst, dst_ref=dst, send_sem=ssem, recv_sem=rsem, device_id=sibling, device_id_type=MESH
        ).wait_recv()

    loads = [
        pltpu.make_async_copy(src, dst, in_sem.at[i])
        for i, (src, dst) in enumerate([
            (resid, resid_v), (gain, gain_v), (encb, encb_v), (frozen, frozen_v), (mgain, mgain_v),
            (enc, enc_v), (dec_s, dec_s_v), (dec_n, dec_n_v), (w_gate, wg_v), (w_up, wu_v), (w_down, wd_v),
        ])
    ]
    for copy in loads:
        copy.start()

    barrier = pltpu.get_barrier_semaphore()
    peers = [sibling, across, across_sib]
    peers += [along_a(d) for d in (1, 2, 3)] + [along_b(d) for d in (1, 2, 3)]
    for dev in peers:
        pl.semaphore_signal(barrier, inc=1, device_id=dev, device_id_type=MESH)
    loads[0].wait()
    lb[core, 0, 0:OWN, :] = resid_v[...]
    lb[core, 0, OWN:PAD, :] = jnp.zeros((PAD - OWN, TOK), BF16)
    pl.semaphore_wait(barrier, len(peers))

    def slot(a, b):
        return (a % 4) * 4 + b % 4

    def push(a, b, da, db):
        dev = along_a(da) if da else along_b(db)
        k = len(sends)
        sends.append(send(
            lb.at[core, slot(a, b)], lb.at[core, slot(a - da, b - db)],
            ag_s.at[k], ag_r.at[slot(a - da, b - db)], dev,
        ))

    def share(a, b):
        s = slot(a, b)
        sends.append(send(lb.at[core, s], lb.at[core, s], d2_s.at[s], d2_r.at[s], sibling))

    for d in (2, 1, 3):
        push(0, 0, d, 0)
    for d in (2, 1, 3):
        push(0, 0, 0, d)
    share(0, 0)

    for copy in loads[1:5]:
        copy.wait()
    for k in range(D // 128):
        gain_b[128 * k:128 * (k + 1), :] = jnp.broadcast_to(gain_v[:, 128 * k:128 * (k + 1)], (128, 128)).T
    for k in range(LAT // 128):
        encb_b[128 * k:128 * (k + 1), :] = jnp.broadcast_to(encb_v[:, 128 * k:128 * (k + 1)], (128, 128)).T
    mg_send[...] = jnp.broadcast_to(mgain_v[...], (128, OWN)).T
    fz_send[0:OWN, :] = frozen_v[:, sib_lanes]
    fz_send[OWN:PAD, :] = jnp.zeros((PAD - OWN, HALF), BF16)

    for a, b in SINGLES_A:
        arrived(lb.at[core, slot(a, b)], ag_s.at[0], ag_r.at[slot(a, b)])
        for d in (2, 1, 3):
            push(a, b, 0, d)
        share(a, b)
    sends.append(send(mg_send, mg_recv, ms_s.at[0], ms_r.at[0], sibling))
    sends.append(send(fz_send, fz_recv, ms_s.at[1], ms_r.at[1], sibling))

    squares = []

    def use(a, b):
        mirror = slot(b, a)
        arrived(lb.at[1 - core, mirror], ag_s.at[0], d2_r.at[mirror])
        slot0 = jnp.where(first, slot(a, b), mirror)
        slot1 = jnp.where(first, mirror, slot(a, b))
        rows = pl.ds(pl.multiple_of(chip_at(a, b) * CHIP, 16), CHIP)
        v = jnp.concatenate([lb[0, slot0, 0:OWN, :].astype(F32), lb[1, slot1, 0:OWN, :].astype(F32)], axis=0)
        squares.append(jnp.sum(v * v, axis=0, keepdims=True))
        g = gain_b[rows, :]
        g1[rows, :] = (v * jnp.concatenate([g, g], axis=1)).astype(BF16)

    use(0, 0)
    for a, b in SINGLES_B:
        arrived(lb.at[core, slot(a, b)], ag_s.at[0], ag_r.at[slot(a, b)])
        share(a, b)
    for a, b in SINGLES_A + SINGLES_B:
        use(a, b)
    pending = []
    for a, b in DIAGONALS:
        arrived(lb.at[core, slot(a, b)], ag_s.at[0], ag_r.at[slot(a, b)])
        share(a, b)
        pending.append((a, b))
        if (b, a) in pending:
            for pair in pending:
                use(*pair)
            pending = []
    total = squares[0]
    for s in squares[1:]:
        total = total + s
    inv = lax.rsqrt(total / D + EPS)

    loads[5].wait()
    pre = lax.dot_general(enc_v[...], g1[...], TN, preferred_element_type=F32)
    bias = encb_b[...]
    lat_v[...] = jnp.maximum(inv * pre + jnp.concatenate([bias, bias], axis=1), 0.0).astype(BF16)

    def project(dec_ref, i):
        for k in range(6):
            cols = slice(384 * k, 384 * (k + 1))
            prod[i, cols, :] = lax.dot_general(dec_ref[:, cols], lat_v[...], TN, preferred_element_type=F32)

    def whole_unit(i, c, lanes):
        rows = pl.ds(pl.multiple_of(c * CHIP, 16), CHIP)
        return prod[i, rows, lanes]

    def split_unit(i, c, lanes):
        low = pl.ds(pl.multiple_of(c * OWN, 8), OWN)
        high = pl.ds(pl.multiple_of(D // 2 + c * OWN, 8), OWN)
        return jnp.concatenate([prod[i, low, lanes], prod[i, high, lanes]], axis=0)

    def hand_over(i, unit):
        out = []
        for a, b in FAR_FIRST:
            s = slot(a, b)
            ys[i, s] = unit(i, chip_at(b, a), sib_lanes).astype(BF16)
            out.append(send(ys.at[i, s], yr.at[i, s], rs_s.at[i, s], rs_d.at[i, s], sibling))
        return out

    def first_axis(i, unit):
        out = []
        for a, b in FAR_FIRST:
            s = slot(a, b)
            arrived(yr.at[i, s], rs_s.at[i, 0], rs_d.at[i, s])
            v = unit(i, chip_at(a, b), own_lanes) + yr[i, s].astype(F32)
            if a:
                s1[i, s] = v.astype(BF16)
                t = slot(-a, b)
                out.append(send(s1.at[i, s], r1.at[i, t], rs_s.at[i, 16 + s], rs_1.at[i, t], along_a(a)))
            else:
                keep[i, b] = v
        return out

    def second_axis(i):
        out = []
        for b in (2, 1, 3, 0):
            v = keep[i, b]
            for a in (1, 3, 2):
                s = slot(a, b)
                arrived(r1.at[i, s], rs_s.at[i, 0], rs_1.at[i, s])
                v = v + r1[i, s].astype(F32)
            if b:
                s2[i, b] = v.astype(BF16)
                t = (4 - b) % 4
                out.append(send(s2.at[i, b], r2.at[i, t], rs_s.at[i, 16 + b], rs_2.at[i, t], along_b(b)))
            else:
                keep[i, 0] = v
        return out

    def collect(i):
        v = keep[i, 0]
        for b in (1, 3, 2):
            arrived(r2.at[i, b], rs_s.at[i, 0], rs_2.at[i, b])
            v = v + r2[i, b].astype(F32)
        return v

    def settle(copies):
        for copy in copies:
            copy.wait_send()

    loads[6].wait()
    loads[7].wait()

    @pl.when(layer == 0)
    def _():
        project(dec_n_v, 1)
        out = hand_over(1, whole_unit)
        project(dec_s_v, 0)
        out += hand_over(0, whole_unit)
        out += first_axis(1, whole_unit)
        out += first_axis(0, whole_unit)
        out += second_axis(1)
        out += second_axis(0)
        part = collect(1)
        keep[1, 0] = part
        z_send[1] = part.astype(BF16)
        out.append(send(z_send.at[1], z_recv.at[1], ms_s.at[3], ms_r.at[3], across))
        part = collect(0)
        keep[0, 0] = part
        z_send[0] = part.astype(BF16)
        out.append(send(z_send.at[0], z_recv.at[0], ms_s.at[2], ms_r.at[2], across))
        arrived(z_recv.at[0], ms_s.at[2], ms_r.at[2])
        keep[0, 1] = keep[1, 0] + z_recv[0].astype(F32)
        settle(out)

    @pl.when(layer == 1)
    def _():
        project(dec_s_v, 0)
        out = hand_over(0, whole_unit)
        out += first_axis(0, whole_unit)
        out += second_axis(0)
        part = collect(0)
        z_send[0] = part.astype(BF16)
        out.append(send(z_send.at[0], z_recv.at[0], ms_s.at[2], ms_r.at[2], across))
        arrived(z_recv.at[1], ms_s.at[3], ms_r.at[3])
        keep[0, 0] = part + z_recv[1].astype(F32)
        arrived(z_recv.at[0], ms_s.at[2], ms_r.at[2])
        keep[0, 1] = z_recv[0].astype(F32)
        settle(out)

    arrived(mg_recv, ms_s.at[0], ms_r.at[0])
    arrived(fz_recv, ms_s.at[1], ms_r.at[1])
    mine = frozen_v[:, own_lanes].astype(F32)
    theirs = fz_recv[0:OWN, :].astype(F32)
    fz = jnp.concatenate([jnp.where(first, mine, theirs), jnp.where(first, theirs, mine)], axis=0)
    mg0, mg1 = mg_send[...], mg_recv[...]
    mg = jnp.concatenate([jnp.where(first, mg0, mg1), jnp.where(first, mg1, mg0)], axis=0)
    mixed = fz + keep[0, 0] + keep[0, 1]

    sq_a[0] = jnp.broadcast_to(jnp.sum(mixed * mixed, axis=0, keepdims=True), (8, HALF))

    def block(a, b):
        return pl.ds(pl.multiple_of(chip_at(a, b) * CHIP, 16), CHIP)

    sends2 = []
    for d in (2, 1, 3):
        sends2.append(send(sq_a.at[0], sq_a.at[4 - d], sq_s.at[d], sq_r.at[4 - d], along_a(d)))
    g2[block(0, 0), own_lanes] = (mixed * mg).astype(BF16)

    def push2(a, b, da, db):
        dev = along_a(da) if da else along_b(db)
        ref = g2.at[block(a, b), own_lanes]
        sends2.append(send(ref, ref, ag2_s.at[len(sends2)], ag2_r.at[slot(a - da, b - db)], dev))

    def share2(a, b):
        ref = g2.at[block(a, b), own_lanes]
        sends2.append(send(ref, ref, ag2_s.at[len(sends2)], ag2_d.at[slot(a, b)], sibling))

    for d in (2, 1, 3):
        push2(0, 0, d, 0)
    for d in (2, 1, 3):
        push2(0, 0, 0, d)
    share2(0, 0)

    rows_own = keep[0, 0]
    low, high = rows_own[0:OWN], rows_own[OWN:CHIP]
    rc_send[0:OWN, :] = jnp.where(first, high, low).astype(BF16)
    rc_send[OWN:PAD, :] = jnp.zeros((PAD - OWN, HALF), BF16)
    sends2.append(send(rc_send, rc_recv, ms_s.at[4], ms_r.at[4], sibling))
    recon_v[:, own_lanes] = jnp.where(first, low, high).astype(BF16)
    lat_t[...] = lat_v[...].T
    lat_copy = pltpu.make_async_copy(lat_t, lat_out, in_sem.at[0])
    lat_copy.start()

    for a, b in SINGLES_A:
        arrived(g2.at[block(a, b), own_lanes], ag_s.at[0], ag2_r.at[slot(a, b)])
        for d in (2, 1, 3):
            push2(a, b, 0, d)
        share2(a, b)
    sq = sq_a[0]
    for d in (1, 3, 2):
        arrived(sq_a.at[d], ag_s.at[0], sq_r.at[d])
        sq = sq + sq_a[d]
    sq_b[0] = sq
    for d in (2, 1, 3):
        sends2.append(send(sq_b.at[0], sq_b.at[4 - d], sq_s.at[4 + d], sq_r.at[8 - d], along_b(d)))
    for a, b in SINGLES_B:
        arrived(g2.at[block(a, b), own_lanes], ag_s.at[0], ag2_r.at[slot(a, b)])
        share2(a, b)
    arrived(rc_recv, ms_s.at[4], ms_r.at[4])
    recon_v[:, sib_lanes] = rc_recv[0:OWN, :]
    recon_copy = pltpu.make_async_copy(recon_v, recon_out, in_sem.at[1])
    recon_copy.start()
    sq = sq_b[0]
    for d in (1, 3, 2):
        arrived(sq_b.at[d], ag_s.at[0], sq_r.at[4 + d])
        sq = sq + sq_b[d]
    sq_d[0] = sq
    sends2.append(send(sq_d.at[0], sq_d.at[1], sq_s.at[8], sq_r.at[8], sibling))
    for a, b in DIAGONALS:
        arrived(g2.at[block(a, b), own_lanes], ag_s.at[0], ag2_r.at[slot(a, b)])
        share2(a, b)
    arrived(sq_d.at[1], ag_s.at[0], sq_r.at[8])
    other = sq_d[1]
    both = jnp.concatenate([jnp.where(first, sq, other), jnp.where(first, other, sq)], axis=1)[0:1]
    scale = lax.rsqrt(both / D + EPS)
    for copy in loads[8:11]:
        copy.wait()
    for a in range(4):
        for b in range(4):
            arrived(g2.at[block(b, a), sib_lanes], ag_s.at[0], ag2_d.at[slot(a, b)])

    gate = scale * lax.dot_general(wg_v[...], g2[...], NN, preferred_element_type=F32)
    up = scale * lax.dot_general(wu_v[...], g2[...], NN, preferred_element_type=F32)
    hidden = (jax.nn.gelu(gate, approximate=True) * up).astype(BF16)
    for k in range(6):
        cols = slice(384 * k, 384 * (k + 1))
        prod[2, cols, :] = lax.dot_general(wd_v[:, cols], hidden, TN, preferred_element_type=F32)
    sends2 += hand_over(2, split_unit)
    sends2 += first_axis(2, split_unit)
    sends2 += second_axis(2)
    part = collect(2)
    low, high = part[0:OWN], part[OWN:CHIP]
    here = jnp.where(layer == 0, low, high)
    there = jnp.where(layer == 0, high, low)
    zero = jnp.zeros((PAD - OWN, HALF), BF16)
    fin_send[1, 0:OWN, :] = there.astype(BF16)
    fin_send[1, OWN:PAD, :] = zero
    sends2.append(send(fin_send.at[1], fin_recv.at[1], ms_s.at[5], ms_r.at[5], across_sib))
    sends2.append(send(fin_send.at[1], fin_recv.at[2], ms_s.at[6], ms_r.at[6], across))
    fin_send[0, 0:OWN, :] = here.astype(BF16)
    fin_send[0, OWN:PAD, :] = zero
    sends2.append(send(fin_send.at[0], fin_recv.at[0], ms_s.at[7], ms_r.at[7], sibling))
    arrived(fin_recv.at[0], ms_s.at[7], ms_r.at[7])
    arrived(fin_recv.at[2], ms_s.at[6], ms_r.at[6])
    arrived(fin_recv.at[1], ms_s.at[5], ms_r.at[5])
    own_half = here + fin_recv[2, 0:OWN, :].astype(F32)
    sib_half = fin_recv[0, 0:OWN, :].astype(F32) + fin_recv[1, 0:OWN, :].astype(F32)
    out_v[:, own_lanes] = jnp.where(first, own_half[0:36], own_half[36:72]).astype(BF16)
    out_v[:, sib_lanes] = jnp.where(first, sib_half[0:36], sib_half[36:72]).astype(BF16)
    out_copy = pltpu.make_async_copy(out_v, mlp_out, in_sem.at[2])
    out_copy.start()
    settle(sends)
    settle(sends2)
    lat_copy.wait()
    recon_copy.wait()
    out_copy.wait()


def per_device(
    resid_in, clt_gain, enc_w, enc_b, dec_same, dec_next, frozen_sum, mlp_gain, w_gate, w_up, w_down
):
    anywhere = pl.BlockSpec(memory_space=pl.ANY)
    dma = pltpu.SemaphoreType.DMA
    vm = pltpu.VMEM
    lat, recon, out = pl.pallas_call(
        kernel,
        out_shape=(
            jax.ShapeDtypeStruct((TOK, LAT), BF16),
            jax.ShapeDtypeStruct((OWN, TOK), BF16),
            jax.ShapeDtypeStruct((36, TOK), BF16),
        ),
        in_specs=[anywhere] * 11,
        out_specs=[anywhere] * 3,
        scratch_shapes=[
            vm((OWN, TOK), BF16), vm((1, D), F32), vm((1, LAT), F32), vm((OWN, TOK), BF16), vm((1, OWN), F32),
            vm((D, LAT), BF16), vm((LAT, D), BF16), vm((LAT, D), BF16),
            vm((CHIP, D), BF16), vm((CHIP, D), BF16), vm((CHIP, D), BF16),
            vm((D, HALF), F32), vm((LAT, HALF), F32), vm((2, 16, PAD, TOK), BF16), vm((D, TOK), BF16),
            vm((LAT, TOK), BF16), vm((TOK, LAT), BF16),
            vm((PAD, HALF), BF16), vm((PAD, HALF), BF16), vm((OWN, HALF), F32), vm((OWN, HALF), F32),
            vm((3, D, TOK), F32), vm((3, 16, CHIP, HALF), BF16), vm((3, 16, CHIP, HALF), BF16),
            vm((3, 4, CHIP, HALF), F32), vm((3, 16, CHIP, HALF), BF16), vm((3, 16, CHIP, HALF), BF16),
            vm((3, 4, CHIP, HALF), BF16), vm((3, 4, CHIP, HALF), BF16),
            vm((2, CHIP, HALF), BF16), vm((2, CHIP, HALF), BF16), vm((PAD, HALF), BF16), vm((PAD, HALF), BF16),
            vm((OWN, TOK), BF16),
            vm((4, 8, HALF), F32), vm((4, 8, HALF), F32), vm((2, 8, HALF), F32), vm((D, TOK), BF16),
            vm((2, PAD, HALF), BF16), vm((3, PAD, HALF), BF16), vm((36, TOK), BF16),
            dma((11,)), dma((32,)), dma((16,)), dma((16,)), dma((16,)),
            dma((3, 32)), dma((3, 16)), dma((3, 16)), dma((3, 4)),
            dma((48,)), dma((16,)), dma((16,)), dma((9,)), dma((9,)), dma((8,)), dma((8,)),
        ],
        compiler_params=pltpu.CompilerParams(
            collective_id=0, has_side_effects=True, vmem_limit_bytes=58 * 2**20
        ),
        cost_estimate=pl.CostEstimate(flops=2 * 10**9, bytes_accessed=10**7, transcendentals=0),
        name="clt_mlp",
    )(
        resid_in[0].T, clt_gain, enc_b, frozen_sum.T, mlp_gain[None],
        enc_w[0], dec_same[0], dec_next, w_gate.T, w_up.T, w_down,
    )
    return (lat[None], recon.T[None], out.T)


def solution(mesh):
    in_specs = (
        P("layer", "token", "latent"),
        P("layer", None),
        P("layer", None, "latent"),
        P("layer", "latent"),
        P("layer", "latent", None),
        P("latent", None),
        P("token", "latent"),
        P("latent"),
        P(None, ("layer", "latent")),
        P(None, ("layer", "latent")),
        P(("layer", "latent"), None),
    )
    out_specs = (
        P("layer", "token", "latent"),
        P("layer", "token", "latent"),
        P("token", ("layer", "latent")),
    )
    return jax.shard_map(
        per_device, mesh=mesh, in_specs=in_specs, out_specs=out_specs, check_vma=False
    )
```

```python
import jax
import jax.numpy as jnp
from jax import lax
from jax.experimental import pallas as pl
from jax.experimental.pallas import tpu as pltpu
from jax.sharding import PartitionSpec as P

D = 2304
TOK = 256
HALF = 128
CHIP = 144
OWN = 72
PAD = 80
LAT = 512
EPS = 1e-06
MESH = pl.DeviceIdType.MESH
F32 = jnp.float32
BF16 = jnp.bfloat16
TN = (((0,), (0,)), ((), ()))
NN = (((1,), (0,)), ((), ()))

SINGLES_A = [(1, 0), (3, 0), (2, 0)]
SINGLES_B = [(0, 1), (0, 3), (0, 2)]
DIAGONALS = [(1, 1), (3, 3), (1, 3), (3, 1), (1, 2), (2, 1), (3, 2), (2, 3), (2, 2)]
FAR_FIRST = [(a, b) for a in (2, 1, 3, 0) for b in (2, 1, 3, 0)]


def kernel(
    resid, gain, encb, frozen, mgain, enc, dec_s, dec_n, w_gate, w_up, w_down,
    lat_out, recon_out, mlp_out,
    resid_v, gain_v, encb_v, frozen_v, mgain_v, enc_v, dec_s_v, dec_n_v, wg_v, wu_v, wd_v,
    gain_b, encb_b, lb, g1, lat_v, lat_t,
    fz_send, fz_recv, mg_send, mg_recv,
    prod, ys, land, keep, s1, s2,
    z_send, z_recv, rc_send, rc_recv, recon_v,
    sq_all, sq_a, sq_b, sq_d, g2, fin_send, fin_recv, out_v,
    in_sem, out_sem, ag_r, ag_d, rs_s, rs_d, rs_1, rs_2, sq_r, ms_s, ms_r,
):
    layer = lax.axis_index("layer")
    q = lax.axis_index("latent")
    core = lax.rem(q, 2)
    chip = lax.div(q, 2)
    cy = lax.rem(chip, 4)
    cx = lax.div(chip, 4)
    first = core == 0

    def chip_at(a, b):
        dx = jnp.where(first, a, b)
        dy = jnp.where(first, b, a)
        return lax.rem(cx + dx, 4) * 4 + lax.rem(cy + dy, 4)

    def along_a(d):
        return {"latent": chip_at(d, 0) * 2 + core}

    def along_b(d):
        return {"latent": chip_at(0, d) * 2 + core}

    sibling = {"latent": chip * 2 + 1 - core}
    across = {"layer": 1 - layer}
    across_sib = {"layer": 1 - layer, "latent": chip * 2 + 1 - core}
    own_lanes = pl.ds(pl.multiple_of(core * HALF, HALF), HALF)
    sib_lanes = pl.ds(pl.multiple_of((1 - core) * HALF, HALF), HALF)

    def send(src, dst, ssem, rsem, dev):
        copy = pltpu.make_async_remote_copy(
            src_ref=src, dst_ref=dst, send_sem=ssem, recv_sem=rsem, device_id=dev, device_id_type=MESH
        )
        copy.start()
        return copy

    def arrived(dst, rsem):
        pltpu.make_async_remote_copy(
            src_ref=dst, dst_ref=dst, send_sem=out_sem.at[0], recv_sem=rsem, device_id=sibling, device_id_type=MESH
        ).wait_recv()

    def all_sent(refs, ssem):
        pltpu.make_async_remote_copy(
            src_ref=refs, dst_ref=refs, send_sem=ssem, recv_sem=ag_r.at[0, 0], device_id=sibling, device_id_type=MESH
        ).wait_send()

    loads = [
        pltpu.make_async_copy(src, dst, in_sem.at[i])
        for i, (src, dst) in enumerate([
            (resid, resid_v), (gain, gain_v), (encb, encb_v), (frozen, frozen_v), (mgain, mgain_v),
            (enc, enc_v), (dec_s, dec_s_v), (dec_n, dec_n_v), (w_gate, wg_v), (w_up, wu_v), (w_down, wd_v),
        ])
    ]
    for copy in loads:
        copy.start()

    barrier = pltpu.get_barrier_semaphore()
    peers = [sibling, across, across_sib]
    peers += [along_a(d) for d in (1, 2, 3)] + [along_b(d) for d in (1, 2, 3)]
    for dev in peers:
        pl.semaphore_signal(barrier, inc=1, device_id=dev, device_id_type=MESH)
    loads[0].wait()
    lb[core * 16, 0:OWN, :] = resid_v[...]
    lb[core * 16, OWN:PAD, :] = jnp.zeros((PAD - OWN, TOK), BF16)
    pl.semaphore_wait(barrier, len(peers))

    def slot(a, b):
        return (a % 4) * 4 + b % 4

    def group(a, b):
        a, b = a % 4, b % 4
        return a - 1 if b == 0 else 3 + a

    def push(a, b, da, db):
        dev = along_a(da) if da else along_b(db)
        send(
            lb.at[core * 16 + slot(a, b)], lb.at[core * 16 + slot(a - da, b - db)],
            out_sem.at[0], ag_r.at[0, group(a - da, b - db)], dev,
        )

    def share(a, b, n, k):
        ref = lb.at[pl.ds(core * 16 + slot(a, b), n)]
        send(ref, ref, out_sem.at[0], ag_d.at[0, k], sibling)

    for d in (2, 1, 3):
        push(0, 0, d, 0)
    for d in (2, 1, 3):
        push(0, 0, 0, d)
    share(0, 0, 1, 0)

    for copy in loads[1:5]:
        copy.wait()
    for k in range(D // 128):
        gain_b[128 * k:128 * (k + 1), :] = jnp.broadcast_to(gain_v[:, 128 * k:128 * (k + 1)], (128, 128)).T
    for k in range(LAT // 128):
        encb_b[128 * k:128 * (k + 1), :] = jnp.broadcast_to(encb_v[:, 128 * k:128 * (k + 1)], (128, 128)).T
    mg_send[...] = jnp.broadcast_to(mgain_v[...], (128, OWN)).T
    fz_send[0:OWN, :] = frozen_v[:, sib_lanes]
    fz_send[OWN:PAD, :] = jnp.zeros((PAD - OWN, HALF), BF16)

    for a, b in SINGLES_A:
        arrived(lb.at[core * 16 + slot(a, b)], ag_r.at[0, group(a, b)])
        for d in (2, 1, 3):
            push(a, b, 0, d)
        share(a, b, 1, a)
    sends = [
        send(mg_send, mg_recv, ms_s.at[0], ms_r.at[0], sibling),
        send(fz_send, fz_recv, ms_s.at[1], ms_r.at[1], sibling),
    ]

    squares = []

    def use(a, b):
        mine, mirror = slot(a, b), slot(b, a)
        slot0 = jnp.where(first, mine, mirror)
        slot1 = jnp.where(first, mirror, mine)
        rows = pl.ds(pl.multiple_of(chip_at(a, b) * CHIP, 16), CHIP)
        v = jnp.concatenate([lb[slot0, 0:OWN, :].astype(F32), lb[16 + slot1, 0:OWN, :].astype(F32)], axis=0)
        squares.append(jnp.sum(v * v, axis=0, keepdims=True))
        g = gain_b[rows, :]
        g1[rows, :] = (v * jnp.concatenate([g, g], axis=1)).astype(BF16)

    def shared(a, b, n, k):
        arrived(lb.at[pl.ds((1 - core) * 16 + slot(a, b), n)], ag_d.at[0, k])

    shared(0, 0, 1, 0)
    use(0, 0)
    arrived(lb.at[pl.ds(core * 16 + 1, 3)], ag_r.at[0, 3])
    share(0, 1, 3, 4)
    shared(0, 1, 3, 4)
    for a, b in SINGLES_A:
        use(a, b)
    for a, b in SINGLES_A:
        shared(a, b, 1, a)
    for a, b in SINGLES_B:
        use(a, b)
    for a in (1, 3, 2):
        arrived(lb.at[pl.ds(core * 16 + slot(a, 1), 3)], ag_r.at[0, 3 + a])
        share(a, 1, 3, 4 + a)
    for a in (1, 3, 2):
        shared(a, 1, 3, 4 + a)
    for a, b in DIAGONALS:
        use(a, b)
    total = squares[0]
    for s in squares[1:]:
        total = total + s
    inv = lax.rsqrt(total / D + EPS)

    loads[5].wait()
    pre = lax.dot_general(enc_v[...], g1[...], TN, preferred_element_type=F32)
    bias = encb_b[...]
    lat_v[...] = jnp.maximum(inv * pre + jnp.concatenate([bias, bias], axis=1), 0.0).astype(BF16)

    def project(dec_ref, i):
        for k in range(6):
            cols = slice(384 * k, 384 * (k + 1))
            prod[i, cols, :] = lax.dot_general(dec_ref[:, cols], lat_v[...], TN, preferred_element_type=F32)

    def whole_unit(i, c, lanes):
        rows = pl.ds(pl.multiple_of(c * CHIP, 16), CHIP)
        return prod[i, rows, lanes]

    def split_unit(i, c, lanes):
        low = pl.ds(pl.multiple_of(c * OWN, 8), OWN)
        high = pl.ds(pl.multiple_of(D // 2 + c * OWN, 8), OWN)
        return jnp.concatenate([prod[i, low, lanes], prod[i, high, lanes]], axis=0)

    def hand_over(i, unit):
        for a in (2, 1, 3, 0):
            for b in range(4):
                ys[i, slot(a, b)] = unit(i, chip_at(b, a), sib_lanes).astype(BF16)
            send(ys.at[i, 4 * a:4 * a + 4], land.at[i, 4 * a:4 * a + 4], rs_s.at[i], rs_d.at[i, a], sibling)

    def first_axis(i, unit):
        for a in (2, 1, 3, 0):
            arrived(land.at[i, 4 * a:4 * a + 4], rs_d.at[i, a])
            for b in (2, 1, 3, 0):
                s = slot(a, b)
                v = unit(i, chip_at(a, b), own_lanes) + land[i, s].astype(F32)
                if a:
                    s1[i, s] = v.astype(BF16)
                    send(s1.at[i, s], land.at[i, 16 + 3 * b + 3 - a], rs_s.at[i], rs_1.at[i, b], along_a(a))
                else:
                    keep[i, b] = v

    def second_axis(i):
        for b in (2, 1, 3, 0):
            at = 16 + 3 * b
            arrived(land.at[i, at:at + 3], rs_1.at[i, b])
            v = keep[i, b] + land[i, at].astype(F32) + land[i, at + 1].astype(F32) + land[i, at + 2].astype(F32)
            if b:
                s2[i, b] = v.astype(BF16)
                send(s2.at[i, b], land.at[i, 28 + 3 - b], rs_s.at[i], rs_2.at[i], along_b(b))
            else:
                keep[i, 0] = v

    def collect(i):
        arrived(land.at[i, 28:31], rs_2.at[i])
        return keep[i, 0] + land[i, 28].astype(F32) + land[i, 29].astype(F32) + land[i, 30].astype(F32)

    def settle(copies):
        for copy in copies:
            copy.wait_send()

    loads[6].wait()
    loads[7].wait()

    @pl.when(layer == 0)
    def _():
        project(dec_n_v, 1)
        hand_over(1, whole_unit)
        project(dec_s_v, 0)
        hand_over(0, whole_unit)
        first_axis(1, whole_unit)
        first_axis(0, whole_unit)
        second_axis(1)
        second_axis(0)
        part = collect(1)
        keep[1, 0] = part
        z_send[1] = part.astype(BF16)
        early = send(z_send.at[1], z_recv.at[1], ms_s.at[3], ms_r.at[3], across)
        part = collect(0)
        keep[0, 0] = part
        z_send[0] = part.astype(BF16)
        last = send(z_send.at[0], z_recv.at[0], ms_s.at[2], ms_r.at[2], across)
        arrived(z_recv.at[0], ms_r.at[2])
        keep[0, 1] = keep[1, 0] + z_recv[0].astype(F32)
        all_sent(land.at[1, 0:31], rs_s.at[1])
        all_sent(land.at[0, 0:31], rs_s.at[0])
        settle([early, last])

    @pl.when(layer == 1)
    def _():
        project(dec_s_v, 0)
        hand_over(0, whole_unit)
        first_axis(0, whole_unit)
        second_axis(0)
        part = collect(0)
        z_send[0] = part.astype(BF16)
        last = send(z_send.at[0], z_recv.at[0], ms_s.at[2], ms_r.at[2], across)
        arrived(z_recv.at[1], ms_r.at[3])
        keep[0, 0] = part + z_recv[1].astype(F32)
        arrived(z_recv.at[0], ms_r.at[2])
        keep[0, 1] = z_recv[0].astype(F32)
        all_sent(land.at[0, 0:31], rs_s.at[0])
        settle([last])

    arrived(mg_recv, ms_r.at[0])
    arrived(fz_recv, ms_r.at[1])
    mine = frozen_v[:, own_lanes].astype(F32)
    theirs = fz_recv[0:OWN, :].astype(F32)
    fz = jnp.concatenate([jnp.where(first, mine, theirs), jnp.where(first, theirs, mine)], axis=0)
    mg0, mg1 = mg_send[...], mg_recv[...]
    mg = jnp.concatenate([jnp.where(first, mg0, mg1), jnp.where(first, mg1, mg0)], axis=0)
    mixed = fz + keep[0, 0] + keep[0, 1]

    sq_a[0] = jnp.broadcast_to(jnp.sum(mixed * mixed, axis=0, keepdims=True), (8, HALF))

    def block(a, b):
        return pl.ds(pl.multiple_of(chip_at(a, b) * CHIP, 16), CHIP)

    sends2 = []
    for d in (2, 1, 3):
        send(sq_a.at[0], sq_a.at[4 - d], out_sem.at[2], sq_r.at[0], along_a(d))
    g2[block(0, 0), own_lanes] = (mixed * mg).astype(BF16)

    def push2(a, b, da, db):
        dev = along_a(da) if da else along_b(db)
        ref = g2.at[block(a, b), own_lanes]
        send(ref, ref, out_sem.at[1], ag_r.at[1, group(a - da, b - db)], dev)

    def share2(a, b, k):
        ref = g2.at[block(a, b), own_lanes]
        send(ref, ref, out_sem.at[1], ag_d.at[1, k], sibling)

    three = land.at[0, 28:31]

    for d in (2, 1, 3):
        push2(0, 0, d, 0)
    for d in (2, 1, 3):
        push2(0, 0, 0, d)
    share2(0, 0, 0)

    rows_own = keep[0, 0]
    low, high = rows_own[0:OWN], rows_own[OWN:CHIP]
    rc_send[0:OWN, :] = jnp.where(first, high, low).astype(BF16)
    rc_send[OWN:PAD, :] = jnp.zeros((PAD - OWN, HALF), BF16)
    sends2.append(send(rc_send, rc_recv, ms_s.at[4], ms_r.at[4], sibling))
    recon_v[:, own_lanes] = jnp.where(first, low, high).astype(BF16)
    lat_t[...] = lat_v[...].T
    lat_copy = pltpu.make_async_copy(lat_t, lat_out, in_sem.at[0])
    lat_copy.start()

    for a, b in SINGLES_A:
        arrived(g2.at[block(a, b), own_lanes], ag_r.at[1, group(a, b)])
        for d in (2, 1, 3):
            push2(a, b, 0, d)
        share2(a, b, a)
    arrived(sq_a.at[1:4], sq_r.at[0])
    sq = sq_a[0] + sq_a[1] + sq_a[2] + sq_a[3]
    sq_b[0] = sq
    for d in (2, 1, 3):
        send(sq_b.at[0], sq_b.at[4 - d], out_sem.at[2], sq_r.at[1], along_b(d))
    arrived(three, ag_r.at[1, 3])
    for a, b in SINGLES_B:
        share2(a, b, 4)
    arrived(rc_recv, ms_r.at[4])
    recon_v[:, sib_lanes] = rc_recv[0:OWN, :]
    recon_copy = pltpu.make_async_copy(recon_v, recon_out, in_sem.at[1])
    recon_copy.start()
    arrived(sq_b.at[1:4], sq_r.at[1])
    sq = sq_b[0] + sq_b[1] + sq_b[2] + sq_b[3]
    sq_d[0] = sq
    send(sq_d.at[0], sq_d.at[1], out_sem.at[2], sq_r.at[2], sibling)
    for a in (1, 3, 2):
        arrived(three, ag_r.at[1, 3 + a])
        for b in (1, 3, 2):
            share2(a, b, 4 + a)
    arrived(sq_d.at[1], sq_r.at[2])
    other = sq_d[1]
    both = jnp.concatenate([jnp.where(first, sq, other), jnp.where(first, other, sq)], axis=1)[0:1]
    scale = lax.rsqrt(both / D + EPS)
    for copy in loads[8:11]:
        copy.wait()
    for k in range(4):
        arrived(land.at[0, 28], ag_d.at[1, k])
    for k in range(4, 8):
        arrived(three, ag_d.at[1, k])

    gate = scale * lax.dot_general(wg_v[...], g2[...], NN, preferred_element_type=F32)
    up = scale * lax.dot_general(wu_v[...], g2[...], NN, preferred_element_type=F32)
    hidden = (jax.nn.gelu(gate, approximate=True) * up).astype(BF16)
    for k in range(6):
        cols = slice(384 * k, 384 * (k + 1))
        prod[2, cols, :] = lax.dot_general(wd_v[:, cols], hidden, TN, preferred_element_type=F32)
    hand_over(2, split_unit)
    first_axis(2, split_unit)
    second_axis(2)
    part = collect(2)
    low, high = part[0:OWN], part[OWN:CHIP]
    here = jnp.where(layer == 0, low, high)
    there = jnp.where(layer == 0, high, low)
    zero = jnp.zeros((PAD - OWN, HALF), BF16)
    fin_send[1, 0:OWN, :] = there.astype(BF16)
    fin_send[1, OWN:PAD, :] = zero
    sends2.append(send(fin_send.at[1], fin_recv.at[1], ms_s.at[5], ms_r.at[5], across_sib))
    sends2.append(send(fin_send.at[1], fin_recv.at[2], ms_s.at[6], ms_r.at[6], across))
    fin_send[0, 0:OWN, :] = here.astype(BF16)
    fin_send[0, OWN:PAD, :] = zero
    sends2.append(send(fin_send.at[0], fin_recv.at[0], ms_s.at[7], ms_r.at[7], sibling))
    arrived(fin_recv.at[0], ms_r.at[7])
    arrived(fin_recv.at[2], ms_r.at[6])
    arrived(fin_recv.at[1], ms_r.at[5])
    own_half = here + fin_recv[2, 0:OWN, :].astype(F32)
    sib_half = fin_recv[0, 0:OWN, :].astype(F32) + fin_recv[1, 0:OWN, :].astype(F32)
    out_v[:, own_lanes] = jnp.where(first, own_half[0:36], own_half[36:72]).astype(BF16)
    out_v[:, sib_lanes] = jnp.where(first, sib_half[0:36], sib_half[36:72]).astype(BF16)
    out_copy = pltpu.make_async_copy(out_v, mlp_out, in_sem.at[2])
    out_copy.start()
    all_sent(lb.at[0:31], out_sem.at[0])
    all_sent(land.at[0, 0:31], out_sem.at[1])
    all_sent(sq_all, out_sem.at[2])
    all_sent(land.at[2, 0:31], rs_s.at[2])
    settle(sends)
    settle(sends2)
    lat_copy.wait()
    recon_copy.wait()
    out_copy.wait()


def write_out(lat, recon, out, lat_out, recon_out, mlp_out, sem):
    copies = [
        pltpu.make_async_copy(src, dst, sem.at[i])
        for i, (src, dst) in enumerate([(lat, lat_out), (recon, recon_out), (out, mlp_out)])
    ]
    for copy in copies:
        copy.start()
    for copy in copies:
        copy.wait()


def per_device(
    resid_in, clt_gain, enc_w, enc_b, dec_same, dec_next, frozen_sum, mlp_gain, w_gate, w_up, w_down
):
    anywhere = pl.BlockSpec(memory_space=pl.ANY)
    dma = pltpu.SemaphoreType.DMA
    vm = pltpu.VMEM
    lat, recon, out = pl.pallas_call(
        kernel,
        out_shape=(
            jax.ShapeDtypeStruct((TOK, LAT), BF16),
            jax.ShapeDtypeStruct((OWN, TOK), BF16),
            jax.ShapeDtypeStruct((36, TOK), BF16),
        ),
        in_specs=[anywhere] * 11,
        out_specs=[anywhere] * 3,
        scratch_shapes=[
            vm((OWN, TOK), BF16), vm((1, D), F32), vm((1, LAT), F32), vm((OWN, TOK), BF16), vm((1, OWN), F32),
            vm((D, LAT), BF16), vm((LAT, D), BF16), vm((LAT, D), BF16),
            vm((CHIP, D), BF16), vm((CHIP, D), BF16), vm((CHIP, D), BF16),
            vm((D, HALF), F32), vm((LAT, HALF), F32), vm((32, PAD, TOK), BF16), vm((D, TOK), BF16),
            vm((LAT, TOK), BF16), vm((TOK, LAT), BF16),
            vm((PAD, HALF), BF16), vm((PAD, HALF), BF16), vm((OWN, HALF), F32), vm((OWN, HALF), F32),
            vm((3, D, TOK), F32), vm((3, 16, CHIP, HALF), BF16), vm((3, 31, CHIP, HALF), BF16),
            vm((3, 4, CHIP, HALF), F32), vm((3, 16, CHIP, HALF), BF16), vm((3, 4, CHIP, HALF), BF16),
            vm((2, CHIP, HALF), BF16), vm((2, CHIP, HALF), BF16), vm((PAD, HALF), BF16), vm((PAD, HALF), BF16),
            vm((OWN, TOK), BF16),
            vm((7, 8, HALF), F32), vm((4, 8, HALF), F32), vm((4, 8, HALF), F32), vm((2, 8, HALF), F32), vm((D, TOK), BF16),
            vm((2, PAD, HALF), BF16), vm((3, PAD, HALF), BF16), vm((36, TOK), BF16),
            dma((11,)), dma((3,)), dma((2, 7)), dma((2, 8)),
            dma((3,)), dma((3, 4)), dma((3, 4)), dma((3,)), dma((3,)), dma((8,)), dma((8,)),
        ],
        compiler_params=pltpu.CompilerParams(
            collective_id=0, has_side_effects=True, vmem_limit_bytes=58 * 2**20
        ),
        cost_estimate=pl.CostEstimate(flops=2 * 10**9, bytes_accessed=10**7, transcendentals=0),
        name="clt_mlp",
    )(
        resid_in[0].T, clt_gain, enc_b, frozen_sum.T, mlp_gain[None],
        enc_w[0], dec_same[0], dec_next, w_gate.T, w_up.T, w_down,
    )
    lat, recon, out = pl.pallas_call(
        write_out,
        out_shape=(
            jax.ShapeDtypeStruct((TOK, LAT), BF16),
            jax.ShapeDtypeStruct((OWN, TOK), BF16),
            jax.ShapeDtypeStruct((36, TOK), BF16),
        ),
        in_specs=[anywhere] * 3,
        out_specs=[anywhere] * 3,
        scratch_shapes=[dma((3,))],
        name="write_out",
    )(lat, recon, out)
    return (lat[None], recon.T[None], out.T)


def solution(mesh):
    in_specs = (
        P("layer", "token", "latent"),
        P("layer", None),
        P("layer", None, "latent"),
        P("layer", "latent"),
        P("layer", "latent", None),
        P("latent", None),
        P("token", "latent"),
        P("latent"),
        P(None, ("layer", "latent")),
        P(None, ("layer", "latent")),
        P(("layer", "latent"), None),
    )
    out_specs = (
        P("layer", "token", "latent"),
        P("layer", "token", "latent"),
        P("token", ("layer", "latent")),
    )
    return jax.shard_map(
        per_device, mesh=mesh, in_specs=in_specs, out_specs=out_specs, check_vma=False
    )
```

```python
import jax
import jax.numpy as jnp
from jax import lax
from jax.experimental import pallas as pl
from jax.experimental.pallas import tpu as pltpu
from jax.sharding import PartitionSpec as P

D = 2304
TOK = 256
HALF = 128
CHIP = 144
OWN = 72
PAD = 80
LAT = 512
EPS = 1e-06
MESH = pl.DeviceIdType.MESH
F32 = jnp.float32
BF16 = jnp.bfloat16
TN = (((0,), (0,)), ((), ()))
NN = (((1,), (0,)), ((), ()))

SINGLES_A = [(1, 0), (3, 0), (2, 0)]
SINGLES_B = [(0, 1), (0, 3), (0, 2)]
DIAGONALS = [(1, 1), (3, 3), (1, 3), (3, 1), (1, 2), (2, 1), (3, 2), (2, 3), (2, 2)]
FAR_FIRST = [(a, b) for a in (2, 1, 3, 0) for b in (2, 1, 3, 0)]


def kernel(
    resid, gain, encb, frozen, mgain, enc, dec_s, dec_n, w_gate, w_up, w_down,
    lat_out, recon_out, mlp_out,
    resid_v, gain_v, encb_v, frozen_v, mgain_v, enc_v, dec_s_v, dec_n_v, wg_v, wu_v, wd_v,
    gain_b, encb_b, lb, g1, lat_v, lat_t,
    fz_send, fz_recv, mg_send, mg_recv,
    prod, ys, land, keep, s1, s2,
    z_send, z_recv, rc_send, rc_recv, recon_v,
    sq_all, sq_a, sq_b, sq_d, g2, fin_send, fin_recv, out_v,
    in_sem, out_sem, ag_r, ag_d, rs_s, rs_d, rs_1, rs_2, sq_r, ms_s, ms_r,
):
    layer = lax.axis_index("layer")
    q = lax.axis_index("latent")
    core = lax.rem(q, 2)
    chip = lax.div(q, 2)
    cy = lax.rem(chip, 4)
    cx = lax.div(chip, 4)
    first = core == 0

    def chip_at(a, b):
        dx = jnp.where(first, a, b)
        dy = jnp.where(first, b, a)
        return lax.rem(cx + dx, 4) * 4 + lax.rem(cy + dy, 4)

    def along_a(d):
        return {"latent": chip_at(d, 0) * 2 + core}

    def along_b(d):
        return {"latent": chip_at(0, d) * 2 + core}

    sibling = {"latent": chip * 2 + 1 - core}
    across = {"layer": 1 - layer}

    def across_b(d):
        return {"layer": 1 - layer, "latent": chip_at(0, d) * 2 + core}

    own_lanes = pl.ds(pl.multiple_of(core * HALF, HALF), HALF)
    sib_lanes = pl.ds(pl.multiple_of((1 - core) * HALF, HALF), HALF)

    def send(src, dst, ssem, rsem, dev):
        copy = pltpu.make_async_remote_copy(
            src_ref=src, dst_ref=dst, send_sem=ssem, recv_sem=rsem, device_id=dev, device_id_type=MESH
        )
        copy.start()
        return copy

    def arrived(dst, rsem):
        pltpu.make_async_remote_copy(
            src_ref=dst, dst_ref=dst, send_sem=out_sem.at[0], recv_sem=rsem, device_id=sibling, device_id_type=MESH
        ).wait_recv()

    def all_sent(refs, ssem):
        pltpu.make_async_remote_copy(
            src_ref=refs, dst_ref=refs, send_sem=ssem, recv_sem=ag_r.at[0, 0], device_id=sibling, device_id_type=MESH
        ).wait_send()

    loads = [
        pltpu.make_async_copy(src, dst, in_sem.at[i])
        for i, (src, dst) in enumerate([
            (resid, resid_v), (gain, gain_v), (encb, encb_v), (frozen, frozen_v), (mgain, mgain_v),
            (enc, enc_v), (dec_s, dec_s_v), (dec_n, dec_n_v), (w_gate, wg_v), (w_up, wu_v), (w_down, wd_v),
        ])
    ]
    for copy in loads:
        copy.start()

    barrier = pltpu.get_barrier_semaphore()
    peers = [sibling, across]
    peers += [f(d) for f in (along_a, along_b, across_b) for d in (1, 2, 3)]
    for dev in peers:
        pl.semaphore_signal(barrier, inc=1, device_id=dev, device_id_type=MESH)
    loads[0].wait()
    lb[core * 16, 0:OWN, :] = resid_v[...]
    lb[core * 16, OWN:PAD, :] = jnp.zeros((PAD - OWN, TOK), BF16)
    pl.semaphore_wait(barrier, len(peers))

    def slot(a, b):
        return (a % 4) * 4 + b % 4

    def group(a, b):
        a, b = a % 4, b % 4
        return a - 1 if b == 0 else 3 + a

    def push(a, b, da, db):
        dev = along_a(da) if da else along_b(db)
        send(
            lb.at[core * 16 + slot(a, b)], lb.at[core * 16 + slot(a - da, b - db)],
            out_sem.at[0], ag_r.at[0, group(a - da, b - db)], dev,
        )

    def share(a, b, n, k):
        ref = lb.at[pl.ds(core * 16 + slot(a, b), n)]
        send(ref, ref, out_sem.at[0], ag_d.at[0, k], sibling)

    for d in (2, 1, 3):
        push(0, 0, d, 0)
    for d in (2, 1, 3):
        push(0, 0, 0, d)
    share(0, 0, 1, 0)

    for copy in loads[1:5]:
        copy.wait()
    for k in range(D // 128):
        gain_b[128 * k:128 * (k + 1), :] = jnp.broadcast_to(gain_v[:, 128 * k:128 * (k + 1)], (128, 128)).T
    for k in range(LAT // 128):
        encb_b[128 * k:128 * (k + 1), :] = jnp.broadcast_to(encb_v[:, 128 * k:128 * (k + 1)], (128, 128)).T
    mg_send[...] = jnp.broadcast_to(mgain_v[...], (128, OWN)).T
    fz_send[0:OWN, :] = frozen_v[:, sib_lanes]
    fz_send[OWN:PAD, :] = jnp.zeros((PAD - OWN, HALF), BF16)

    for a, b in SINGLES_A:
        arrived(lb.at[core * 16 + slot(a, b)], ag_r.at[0, group(a, b)])
        for d in (2, 1, 3):
            push(a, b, 0, d)
        share(a, b, 1, a)
    sends = [
        send(mg_send, mg_recv, ms_s.at[0], ms_r.at[0], sibling),
        send(fz_send, fz_recv, ms_s.at[1], ms_r.at[1], sibling),
    ]

    squares = []

    def use(a, b):
        mine, mirror = slot(a, b), slot(b, a)
        slot0 = jnp.where(first, mine, mirror)
        slot1 = jnp.where(first, mirror, mine)
        rows = pl.ds(pl.multiple_of(chip_at(a, b) * CHIP, 16), CHIP)
        v = jnp.concatenate([lb[slot0, 0:OWN, :].astype(F32), lb[16 + slot1, 0:OWN, :].astype(F32)], axis=0)
        squares.append(jnp.sum(v * v, axis=0, keepdims=True))
        g = gain_b[rows, :]
        g1[rows, :] = (v * jnp.concatenate([g, g], axis=1)).astype(BF16)

    def shared(a, b, n, k):
        arrived(lb.at[pl.ds((1 - core) * 16 + slot(a, b), n)], ag_d.at[0, k])

    shared(0, 0, 1, 0)
    use(0, 0)
    arrived(lb.at[pl.ds(core * 16 + 1, 3)], ag_r.at[0, 3])
    share(0, 1, 3, 4)
    shared(0, 1, 3, 4)
    for a, b in SINGLES_A:
        use(a, b)
    for a, b in SINGLES_A:
        shared(a, b, 1, a)
    for a, b in SINGLES_B:
        use(a, b)
    for a in (1, 3, 2):
        arrived(lb.at[pl.ds(core * 16 + slot(a, 1), 3)], ag_r.at[0, 3 + a])
        share(a, 1, 3, 4 + a)
    for a in (1, 3, 2):
        shared(a, 1, 3, 4 + a)
    for a, b in DIAGONALS:
        use(a, b)
    total = squares[0]
    for s in squares[1:]:
        total = total + s
    inv = lax.rsqrt(total / D + EPS)

    loads[5].wait()
    pre = lax.dot_general(enc_v[...], g1[...], TN, preferred_element_type=F32)
    bias = encb_b[...]
    lat_v[...] = jnp.maximum(inv * pre + jnp.concatenate([bias, bias], axis=1), 0.0).astype(BF16)

    def project(dec_ref, i, base=None):
        for k in range(6):
            cols = slice(384 * k, 384 * (k + 1))
            v = lax.dot_general(dec_ref[:, cols], lat_v[...], TN, preferred_element_type=F32)
            prod[i, cols, :] = v if base is None else v + prod[base, cols, :]

    def whole_unit(i, c, lanes):
        rows = pl.ds(pl.multiple_of(c * CHIP, 16), CHIP)
        return prod[i, rows, lanes]

    def split_unit(i, c, lanes):
        low = pl.ds(pl.multiple_of(c * OWN, 8), OWN)
        high = pl.ds(pl.multiple_of(D // 2 + c * OWN, 8), OWN)
        return jnp.concatenate([prod[i, low, lanes], prod[i, high, lanes]], axis=0)

    def hand_over(i, unit):
        for a in (2, 1, 3, 0):
            for b in range(4):
                ys[i, slot(a, b)] = unit(i, chip_at(b, a), sib_lanes).astype(BF16)
            send(ys.at[i, 4 * a:4 * a + 4], land.at[i, 4 * a:4 * a + 4], rs_s.at[i], rs_d.at[i, a], sibling)

    def first_axis(i, unit):
        for a in (2, 1, 3, 0):
            arrived(land.at[i, 4 * a:4 * a + 4], rs_d.at[i, a])
            for b in (2, 1, 3, 0):
                s = slot(a, b)
                v = unit(i, chip_at(a, b), own_lanes) + land[i, s].astype(F32)
                if a:
                    s1[i, s] = v.astype(BF16)
                    send(s1.at[i, s], land.at[i, 16 + 3 * b + 3 - a], rs_s.at[i], rs_1.at[i, b], along_a(a))
                else:
                    keep[i, b] = v

    def second_axis(i):
        for b in (2, 1, 3, 0):
            at = 16 + 3 * b
            arrived(land.at[i, at:at + 3], rs_1.at[i, b])
            v = keep[i, b] + land[i, at].astype(F32) + land[i, at + 1].astype(F32) + land[i, at + 2].astype(F32)
            if b:
                s2[i, b] = v.astype(BF16)
                send(s2.at[i, b], land.at[i, 28 + 3 - b], rs_s.at[i], rs_2.at[i], along_b(b))
            else:
                keep[i, 0] = v

    def collect(i):
        arrived(land.at[i, 28:31], rs_2.at[i])
        return keep[i, 0] + land[i, 28].astype(F32) + land[i, 29].astype(F32) + land[i, 30].astype(F32)

    def settle(copies):
        for copy in copies:
            copy.wait_send()

    loads[6].wait()
    loads[7].wait()

    @pl.when(layer == 0)
    def _():
        project(dec_s_v, 0)
        project(dec_n_v, 1, base=0)

    @pl.when(layer == 1)
    def _():
        project(dec_s_v, 1)

    hand_over(1, whole_unit)

    @pl.when(layer == 0)
    def _():
        hand_over(0, whole_unit)

    first_axis(1, whole_unit)
    second_axis(1)

    @pl.when(layer == 0)
    def _():
        first_axis(0, whole_unit)

    part = collect(1)
    z_send[0] = part.astype(BF16)
    sends.append(send(z_send.at[0], z_recv.at[0], ms_s.at[2], ms_r.at[2], across))
    keep[1, 0] = part
    arrived(mg_recv, ms_r.at[0])
    arrived(fz_recv, ms_r.at[1])
    mine = frozen_v[:, own_lanes].astype(F32)
    theirs = fz_recv[0:OWN, :].astype(F32)
    fz = jnp.concatenate([jnp.where(first, mine, theirs), jnp.where(first, theirs, mine)], axis=0)
    mg0, mg1 = mg_send[...], mg_recv[...]
    mg = jnp.concatenate([jnp.where(first, mg0, mg1), jnp.where(first, mg1, mg0)], axis=0)
    arrived(z_recv.at[0], ms_r.at[2])
    mixed = fz + keep[1, 0] + z_recv[0].astype(F32)

    sq_a[0] = jnp.broadcast_to(jnp.sum(mixed * mixed, axis=0, keepdims=True), (8, HALF))

    def block(a, b):
        return pl.ds(pl.multiple_of(chip_at(a, b) * CHIP, 16), CHIP)

    sends2 = []
    for d in (2, 1, 3):
        send(sq_a.at[0], sq_a.at[4 - d], out_sem.at[2], sq_r.at[0], along_a(d))
    g2[block(0, 0), own_lanes] = (mixed * mg).astype(BF16)

    def push2(a, b, da, db):
        dev = along_a(da) if da else along_b(db)
        ref = g2.at[block(a, b), own_lanes]
        send(ref, ref, out_sem.at[1], ag_r.at[1, group(a - da, b - db)], dev)

    def share2(a, b, k):
        ref = g2.at[block(a, b), own_lanes]
        send(ref, ref, out_sem.at[1], ag_d.at[1, k], sibling)

    three = land.at[0, 28:31]

    for d in (2, 1, 3):
        push2(0, 0, d, 0)
    for d in (2, 1, 3):
        push2(0, 0, 0, d)
    share2(0, 0, 0)

    lat_t[...] = lat_v[...].T
    lat_copy = pltpu.make_async_copy(lat_t, lat_out, in_sem.at[0])
    lat_copy.start()

    for a, b in SINGLES_A:
        arrived(g2.at[block(a, b), own_lanes], ag_r.at[1, group(a, b)])
        for d in (2, 1, 3):
            push2(a, b, 0, d)
        share2(a, b, a)

    @pl.when(layer == 0)
    def _():
        second_axis(0)

    arrived(sq_a.at[1:4], sq_r.at[0])
    sq = sq_a[0] + sq_a[1] + sq_a[2] + sq_a[3]
    sq_b[0] = sq
    for d in (2, 1, 3):
        send(sq_b.at[0], sq_b.at[4 - d], out_sem.at[2], sq_r.at[1], along_b(d))
    arrived(three, ag_r.at[1, 3])
    for a, b in SINGLES_B:
        share2(a, b, 4)
    arrived(sq_b.at[1:4], sq_r.at[1])
    sq = sq_b[0] + sq_b[1] + sq_b[2] + sq_b[3]
    sq_d[0] = sq
    send(sq_d.at[0], sq_d.at[1], out_sem.at[2], sq_r.at[2], sibling)
    for a in (1, 3, 2):
        arrived(three, ag_r.at[1, 3 + a])
        for b in (1, 3, 2):
            share2(a, b, 4 + a)
    arrived(sq_d.at[1], sq_r.at[2])
    other = sq_d[1]
    both = jnp.concatenate([jnp.where(first, sq, other), jnp.where(first, other, sq)], axis=1)[0:1]
    scale = lax.rsqrt(both / D + EPS)

    for copy in loads[8:11]:
        copy.wait()
    for k in range(4):
        arrived(land.at[0, 28], ag_d.at[1, k])
    for k in range(4, 8):
        arrived(three, ag_d.at[1, k])

    gate = scale * lax.dot_general(wg_v[...], g2[...], NN, preferred_element_type=F32)
    up = scale * lax.dot_general(wu_v[...], g2[...], NN, preferred_element_type=F32)
    hidden = (jax.nn.gelu(gate, approximate=True) * up).astype(BF16)
    for k in range(6):
        cols = slice(384 * k, 384 * (k + 1))
        prod[2, cols, :] = lax.dot_general(wd_v[:, cols], hidden, TN, preferred_element_type=F32)
    hand_over(2, split_unit)

    @pl.when(layer == 0)
    def _():
        own = collect(0)
        z_send[1] = (keep[1, 0] - own).astype(BF16)
        send(z_send.at[1], z_recv.at[1], ms_s.at[3], ms_r.at[3], across)
        keep[1, 0] = own

    first_axis(2, split_unit)

    zero = jnp.zeros((PAD - OWN, HALF), BF16)

    for b in (2, 1, 3, 0):
        at = 16 + 3 * b
        arrived(land.at[2, at:at + 3], rs_1.at[2, b])
        v = keep[2, b] + land[2, at].astype(F32) + land[2, at + 1].astype(F32) + land[2, at + 2].astype(F32)
        low, high = v[0:OWN], v[OWN:CHIP]
        here = jnp.where(layer == 0, low, high)
        there = jnp.where(layer == 0, high, low)
        fin_send[b, 0:OWN, :] = there.astype(BF16)
        fin_send[b, OWN:PAD, :] = zero
        send(fin_send.at[b], fin_recv.at[(4 - b) % 4], rs_s.at[3], rs_2.at[2], across_b(b) if b else across)
        if b:
            fin_send[3 + b, 0:OWN, :] = here.astype(BF16)
            fin_send[3 + b, OWN:PAD, :] = zero
            send(fin_send.at[3 + b], fin_recv.at[7 - b], rs_s.at[3], rs_2.at[2], along_b(b))

    @pl.when(layer == 1)
    def _():
        arrived(z_recv.at[1], ms_r.at[3])
        keep[1, 0] = keep[1, 0] + z_recv[1].astype(F32)

    low, high = keep[1, 0, 0:OWN, :], keep[1, 0, OWN:CHIP, :]
    rc_send[0:OWN, :] = jnp.where(first, high, low).astype(BF16)
    rc_send[OWN:PAD, :] = zero
    sends2.append(send(rc_send, rc_recv, ms_s.at[4], ms_r.at[4], sibling))
    recon_v[:, own_lanes] = jnp.where(first, low, high).astype(BF16)
    arrived(fin_recv.at[0:7], rs_2.at[2])
    for k in range(7):
        here = here + fin_recv[k, 0:OWN, :].astype(F32)
    fin_send[7, 0:OWN, :] = here.astype(BF16)
    fin_send[7, OWN:PAD, :] = zero
    sends2.append(send(fin_send.at[7], fin_recv.at[7], ms_s.at[5], ms_r.at[5], sibling))
    out_v[:, own_lanes] = jnp.where(first, here[0:36], here[36:72]).astype(BF16)
    arrived(rc_recv, ms_r.at[4])
    recon_v[:, sib_lanes] = rc_recv[0:OWN, :]
    recon_copy = pltpu.make_async_copy(recon_v, recon_out, in_sem.at[1])
    recon_copy.start()
    arrived(fin_recv.at[7], ms_r.at[5])
    sib_half = fin_recv[7, 0:OWN, :].astype(F32)
    out_v[:, sib_lanes] = jnp.where(first, sib_half[0:36], sib_half[36:72]).astype(BF16)
    out_copy = pltpu.make_async_copy(out_v, mlp_out, in_sem.at[2])
    out_copy.start()
    all_sent(lb.at[0:31], out_sem.at[0])
    all_sent(land.at[0, 0:31], out_sem.at[1])
    all_sent(sq_all, out_sem.at[2])
    all_sent(land.at[1, 0:31], rs_s.at[1])
    all_sent(land.at[2, 0:28], rs_s.at[2])
    all_sent(fin_send.at[0:7], rs_s.at[3])

    @pl.when(layer == 0)
    def _():
        all_sent(land.at[0, 0:31], rs_s.at[0])
        all_sent(z_send.at[1], ms_s.at[3])

    settle(sends)
    settle(sends2)
    lat_copy.wait()
    recon_copy.wait()
    out_copy.wait()


def write_out(lat, recon, out, lat_out, recon_out, mlp_out):
    lat_out[...] = lat[...]
    recon_out[...] = recon[...]
    mlp_out[...] = out[...]


def per_device(
    resid_in, clt_gain, enc_w, enc_b, dec_same, dec_next, frozen_sum, mlp_gain, w_gate, w_up, w_down
):
    anywhere = pl.BlockSpec(memory_space=pl.ANY)
    dma = pltpu.SemaphoreType.DMA
    vm = pltpu.VMEM
    lat, recon, out = pl.pallas_call(
        kernel,
        out_shape=(
            jax.ShapeDtypeStruct((TOK, LAT), BF16),
            jax.ShapeDtypeStruct((OWN, TOK), BF16),
            jax.ShapeDtypeStruct((36, TOK), BF16),
        ),
        in_specs=[anywhere] * 11,
        out_specs=[anywhere] * 3,
        scratch_shapes=[
            vm((OWN, TOK), BF16), vm((1, D), F32), vm((1, LAT), F32), vm((OWN, TOK), BF16), vm((1, OWN), F32),
            vm((D, LAT), BF16), vm((LAT, D), BF16), vm((LAT, D), BF16),
            vm((CHIP, D), BF16), vm((CHIP, D), BF16), vm((CHIP, D), BF16),
            vm((D, HALF), F32), vm((LAT, HALF), F32), vm((32, PAD, TOK), BF16), vm((D, TOK), BF16),
            vm((LAT, TOK), BF16), vm((TOK, LAT), BF16),
            vm((PAD, HALF), BF16), vm((PAD, HALF), BF16), vm((OWN, HALF), F32), vm((OWN, HALF), F32),
            vm((3, D, TOK), F32), vm((3, 16, CHIP, HALF), BF16), vm((3, 31, CHIP, HALF), BF16),
            vm((3, 4, CHIP, HALF), F32), vm((3, 16, CHIP, HALF), BF16), vm((3, 4, CHIP, HALF), BF16),
            vm((2, CHIP, HALF), BF16), vm((2, CHIP, HALF), BF16), vm((PAD, HALF), BF16), vm((PAD, HALF), BF16),
            vm((OWN, TOK), BF16),
            vm((7, 8, HALF), F32), vm((4, 8, HALF), F32), vm((4, 8, HALF), F32), vm((2, 8, HALF), F32), vm((D, TOK), BF16),
            vm((8, PAD, HALF), BF16), vm((8, PAD, HALF), BF16), vm((36, TOK), BF16),
            dma((11,)), dma((3,)), dma((2, 7)), dma((2, 8)),
            dma((4,)), dma((3, 4)), dma((3, 4)), dma((3,)), dma((3,)), dma((6,)), dma((6,)),
        ],
        compiler_params=pltpu.CompilerParams(
            collective_id=0, has_side_effects=True, vmem_limit_bytes=58 * 2**20
        ),
        cost_estimate=pl.CostEstimate(flops=2 * 10**9, bytes_accessed=10**7, transcendentals=0),
        name="clt_mlp",
    )(
        resid_in[0].T, clt_gain, enc_b, frozen_sum.T, mlp_gain[None],
        enc_w[0], dec_same[0], dec_next, w_gate.T, w_up.T, w_down,
    )
    lat, recon, out = pl.pallas_call(
        write_out,
        out_shape=(
            jax.ShapeDtypeStruct((TOK, LAT), BF16),
            jax.ShapeDtypeStruct((OWN, TOK), BF16),
            jax.ShapeDtypeStruct((36, TOK), BF16),
        ),
        in_specs=[pl.BlockSpec(memory_space=pltpu.VMEM)] * 3,
        out_specs=[pl.BlockSpec(memory_space=pltpu.VMEM)] * 3,
        name="write_out",
    )(lat, recon, out)
    return (lat[None], recon.T[None], out.T)


def solution(mesh):
    in_specs = (
        P("layer", "token", "latent"),
        P("layer", None),
        P("layer", None, "latent"),
        P("layer", "latent"),
        P("layer", "latent", None),
        P("latent", None),
        P("token", "latent"),
        P("latent"),
        P(None, ("layer", "latent")),
        P(None, ("layer", "latent")),
        P(("layer", "latent"), None),
    )
    out_specs = (
        P("layer", "token", "latent"),
        P("layer", "token", "latent"),
        P("token", ("layer", "latent")),
    )
    return jax.shard_map(
        per_device, mesh=mesh, in_specs=in_specs, out_specs=out_specs, check_vma=False
    )
```

```python
import jax
import jax.numpy as jnp
from jax import lax
from jax.experimental import pallas as pl
from jax.experimental.pallas import tpu as pltpu
from jax.sharding import PartitionSpec as P

D = 2304
TOK = 256
HALF = 128
CHIP = 144
OWN = 72
PAD = 80
LAT = 512
EPS = 1e-06
MESH = pl.DeviceIdType.MESH
F32 = jnp.float32
BF16 = jnp.bfloat16
TN = (((0,), (0,)), ((), ()))
NN = (((1,), (0,)), ((), ()))

SINGLES_A = [(1, 0), (3, 0), (2, 0)]
SINGLES_B = [(0, 1), (0, 3), (0, 2)]
DIAGONALS = [(1, 1), (3, 3), (1, 3), (3, 1), (1, 2), (2, 1), (3, 2), (2, 3), (2, 2)]
FAR_FIRST = [(a, b) for a in (2, 1, 3, 0) for b in (2, 1, 3, 0)]


def kernel(
    resid, gain, encb, frozen, mgain, enc, dec_s, dec_n, w_gate, w_up, w_down,
    lat_out, recon_out, mlp_out,
    resid_v, gain_v, encb_v, frozen_v, mgain_v, enc_v, dec_s_v, dec_n_v, wg_v, wu_v, wd_v,
    gain_b, encb_b, lb, g1, lat_v, lat_t,
    fz_send, fz_recv, mg_send, mg_recv,
    prod, ys, land, keep, s1, s2,
    z_send, z_recv, rc_send, rc_recv, recon_v,
    sq_all, sq_a, sq_b, sq_d, g2, fin_send, fin_recv, out_v,
    in_sem, out_sem, ag_r, ag_d, rs_s, rs_d, rs_1, rs_2, rs_x, sq_r, ms_s, ms_r,
):
    layer = lax.axis_index("layer")
    q = lax.axis_index("latent")
    core = lax.rem(q, 2)
    chip = lax.div(q, 2)
    cy = lax.rem(chip, 4)
    cx = lax.div(chip, 4)
    first = core == 0

    def chip_at(a, b):
        dx = jnp.where(first, a, b)
        dy = jnp.where(first, b, a)
        return lax.rem(cx + dx, 4) * 4 + lax.rem(cy + dy, 4)

    def along_a(d):
        return {"latent": chip_at(d, 0) * 2 + core}

    def along_b(d):
        return {"latent": chip_at(0, d) * 2 + core}

    sibling = {"latent": chip * 2 + 1 - core}
    across = {"layer": 1 - layer}

    def across_b(d):
        return {"layer": 1 - layer, "latent": chip_at(0, d) * 2 + core}

    own_lanes = pl.ds(pl.multiple_of(core * HALF, HALF), HALF)
    sib_lanes = pl.ds(pl.multiple_of((1 - core) * HALF, HALF), HALF)

    def send(src, dst, ssem, rsem, dev):
        copy = pltpu.make_async_remote_copy(
            src_ref=src, dst_ref=dst, send_sem=ssem, recv_sem=rsem, device_id=dev, device_id_type=MESH
        )
        copy.start()
        return copy

    def arrived(dst, rsem):
        pltpu.make_async_remote_copy(
            src_ref=dst, dst_ref=dst, send_sem=out_sem.at[0], recv_sem=rsem, device_id=sibling, device_id_type=MESH
        ).wait_recv()

    def all_sent(refs, ssem):
        pltpu.make_async_remote_copy(
            src_ref=refs, dst_ref=refs, send_sem=ssem, recv_sem=ag_r.at[0, 0], device_id=sibling, device_id_type=MESH
        ).wait_send()

    loads = [
        pltpu.make_async_copy(src, dst, in_sem.at[i])
        for i, (src, dst) in enumerate([
            (resid, resid_v), (gain, gain_v), (encb, encb_v), (frozen, frozen_v), (mgain, mgain_v),
            (enc, enc_v), (dec_s, dec_s_v), (dec_n, dec_n_v), (w_gate, wg_v), (w_up, wu_v), (w_down, wd_v),
        ])
    ]
    for copy in loads:
        copy.start()

    barrier = pltpu.get_barrier_semaphore()
    peers = [sibling, across]
    peers += [f(d) for f in (along_a, along_b, across_b) for d in (1, 2, 3)]
    for dev in peers:
        pl.semaphore_signal(barrier, inc=1, device_id=dev, device_id_type=MESH)
    loads[0].wait()
    lb[core * 16, 0:OWN, :] = resid_v[...]
    lb[core * 16, OWN:PAD, :] = jnp.zeros((PAD - OWN, TOK), BF16)
    pl.semaphore_wait(barrier, len(peers))

    def slot(a, b):
        return (a % 4) * 4 + b % 4

    def group(a, b):
        a, b = a % 4, b % 4
        return a - 1 if b == 0 else 3 + a

    def push(a, b, da, db):
        dev = along_a(da) if da else along_b(db)
        send(
            lb.at[core * 16 + slot(a, b)], lb.at[core * 16 + slot(a - da, b - db)],
            out_sem.at[0], ag_r.at[0, group(a - da, b - db)], dev,
        )

    def share(a, b, n, k):
        ref = lb.at[pl.ds(core * 16 + slot(a, b), n)]
        send(ref, ref, out_sem.at[0], ag_d.at[0, k], sibling)

    for d in (2, 1, 3):
        push(0, 0, d, 0)
    for d in (2, 1, 3):
        push(0, 0, 0, d)
    share(0, 0, 1, 0)

    for copy in loads[1:5]:
        copy.wait()
    for k in range(D // 128):
        gain_b[128 * k:128 * (k + 1), :] = jnp.broadcast_to(gain_v[:, 128 * k:128 * (k + 1)], (128, 128)).T
    for k in range(LAT // 128):
        encb_b[128 * k:128 * (k + 1), :] = jnp.broadcast_to(encb_v[:, 128 * k:128 * (k + 1)], (128, 128)).T
    mg_send[...] = jnp.broadcast_to(mgain_v[...], (128, OWN)).T
    fz_send[0:OWN, :] = frozen_v[:, sib_lanes]
    fz_send[OWN:PAD, :] = jnp.zeros((PAD - OWN, HALF), BF16)

    for a, b in SINGLES_A:
        arrived(lb.at[core * 16 + slot(a, b)], ag_r.at[0, group(a, b)])
        for d in (2, 1, 3):
            push(a, b, 0, d)
        share(a, b, 1, a)
    sends = [
        send(mg_send, mg_recv, ms_s.at[0], ms_r.at[0], sibling),
        send(fz_send, fz_recv, ms_s.at[1], ms_r.at[1], sibling),
    ]

    squares = []

    def use(a, b):
        mine, mirror = slot(a, b), slot(b, a)
        slot0 = jnp.where(first, mine, mirror)
        slot1 = jnp.where(first, mirror, mine)
        rows = pl.ds(pl.multiple_of(chip_at(a, b) * CHIP, 16), CHIP)
        v = jnp.concatenate([lb[slot0, 0:OWN, :].astype(F32), lb[16 + slot1, 0:OWN, :].astype(F32)], axis=0)
        squares.append(jnp.sum(v * v, axis=0, keepdims=True))
        g = gain_b[rows, :]
        g1[rows, :] = (v * jnp.concatenate([g, g], axis=1)).astype(BF16)

    def shared(a, b, n, k):
        arrived(lb.at[pl.ds((1 - core) * 16 + slot(a, b), n)], ag_d.at[0, k])

    shared(0, 0, 1, 0)
    use(0, 0)
    arrived(lb.at[pl.ds(core * 16 + 1, 3)], ag_r.at[0, 3])
    share(0, 1, 3, 4)
    shared(0, 1, 3, 4)
    for a, b in SINGLES_A:
        use(a, b)
    for a, b in SINGLES_A:
        shared(a, b, 1, a)
    for a, b in SINGLES_B:
        use(a, b)

    loads[6].wait()
    loads[7].wait()

    @pl.when(layer == 0)
    def _():
        dec_n_v[...] = dec_n_v[...] + dec_s_v[...]

    for a in (1, 3):
        arrived(lb.at[pl.ds(core * 16 + slot(a, 1), 3)], ag_r.at[0, 3 + a])
        share(a, 1, 3, 4 + a)
    for a in (1, 3):
        shared(a, 1, 3, 4 + a)
    for a, b in DIAGONALS[:4]:
        use(a, b)
    arrived(lb.at[pl.ds(core * 16 + slot(2, 1), 3)], ag_r.at[0, 5])
    share(2, 1, 3, 6)
    shared(2, 1, 3, 6)
    for a, b in DIAGONALS[4:]:
        use(a, b)
    total = squares[0]
    for s in squares[1:]:
        total = total + s
    inv = lax.rsqrt(total / D + EPS)

    loads[5].wait()
    pre = lax.dot_general(enc_v[...], g1[...], TN, preferred_element_type=F32)
    bias = encb_b[...]
    lat_v[...] = jnp.maximum(inv * pre + jnp.concatenate([bias, bias], axis=1), 0.0).astype(BF16)

    def project(dec_ref, i):
        for k in range(6):
            cols = slice(384 * k, 384 * (k + 1))
            prod[i, cols, :] = lax.dot_general(dec_ref[:, cols], lat_v[...], TN, preferred_element_type=F32)

    def whole_unit(i, c, lanes):
        rows = pl.ds(pl.multiple_of(c * CHIP, 16), CHIP)
        return prod[i, rows, lanes]

    def split_unit(i, c, lanes):
        low = pl.ds(pl.multiple_of(c * OWN, 8), OWN)
        high = pl.ds(pl.multiple_of(D // 2 + c * OWN, 8), OWN)
        return jnp.concatenate([prod[i, low, lanes], prod[i, high, lanes]], axis=0)

    def hand_over(i, unit):
        for b in (2, 1, 3, 0):
            for a in range(4):
                ys[i, 4 * b + a] = unit(i, chip_at(b, a), sib_lanes).astype(BF16)
            send(ys.at[i, 4 * b:4 * b + 4], land.at[i, 4 * b:4 * b + 4], rs_s.at[i], rs_d.at[i, b], sibling)

    def first_axis(i, unit):
        for b in (2, 1, 3, 0):
            arrived(land.at[i, 4 * b:4 * b + 4], rs_d.at[i, b])
            for a in (2, 1, 3, 0):
                s = 4 * b + a
                v = unit(i, chip_at(a, b), own_lanes) + land[i, s].astype(F32)
                if a:
                    s1[i, s] = v.astype(BF16)
                    send(s1.at[i, s], land.at[i, 16 + 3 * b + 3 - a], rs_s.at[i], rs_1.at[i, b], along_a(a))
                else:
                    keep[i, b] = v

    def line_sum(i, b):
        at = 16 + 3 * b
        arrived(land.at[i, at:at + 3], rs_1.at[i, b])
        return keep[i, b] + land[i, at].astype(F32) + land[i, at + 1].astype(F32) + land[i, at + 2].astype(F32)

    def second_axis(i, both_layers):
        for b in (2, 1, 3, 0):
            v = line_sum(i, b)
            if b or both_layers:
                s2[i, b] = v.astype(BF16)
            if both_layers:
                dev = across_b(b) if b else across
                send(s2.at[i, b], land.at[i, 31 + (4 - b) % 4], rs_s.at[i], rs_x.at[0], dev)
            if b:
                send(s2.at[i, b], land.at[i, 28 + 3 - b], rs_s.at[i], rs_2.at[i], along_b(b))
            else:
                keep[i, 0] = v

    def collect(i):
        arrived(land.at[i, 28:31], rs_2.at[i])
        return keep[i, 0] + land[i, 28].astype(F32) + land[i, 29].astype(F32) + land[i, 30].astype(F32)

    def settle(copies):
        for copy in copies:
            copy.wait_send()

    @pl.when(layer == 0)
    def _():
        project(dec_n_v, 1)

    @pl.when(layer == 1)
    def _():
        project(dec_s_v, 1)

    hand_over(1, whole_unit)

    @pl.when(layer == 0)
    def _():
        project(dec_s_v, 0)
        hand_over(0, whole_unit)

    first_axis(1, whole_unit)
    second_axis(1, True)

    @pl.when(layer == 0)
    def _():
        first_axis(0, whole_unit)

    arrived(mg_recv, ms_r.at[0])
    arrived(fz_recv, ms_r.at[1])
    mine = frozen_v[:, own_lanes].astype(F32)
    theirs = fz_recv[0:OWN, :].astype(F32)
    fz = jnp.concatenate([jnp.where(first, mine, theirs), jnp.where(first, theirs, mine)], axis=0)
    mg0, mg1 = mg_send[...], mg_recv[...]
    mg = jnp.concatenate([jnp.where(first, mg0, mg1), jnp.where(first, mg1, mg0)], axis=0)
    part = collect(1)
    keep[1, 0] = part
    arrived(land.at[1, 31:35], rs_x.at[0])
    other = land[1, 31].astype(F32) + land[1, 32].astype(F32) + land[1, 33].astype(F32) + land[1, 34].astype(F32)
    mixed = fz + part + other

    sq_a[0] = jnp.broadcast_to(jnp.sum(mixed * mixed, axis=0, keepdims=True), (8, HALF))

    def block(a, b):
        return pl.ds(pl.multiple_of(chip_at(a, b) * CHIP, 16), CHIP)

    sends2 = []
    for d in (2, 1, 3):
        send(sq_a.at[0], sq_a.at[4 - d], out_sem.at[2], sq_r.at[0], along_a(d))
    g2[block(0, 0), own_lanes] = (mixed * mg).astype(BF16)

    def push2(a, b, da, db):
        dev = along_a(da) if da else along_b(db)
        ref = g2.at[block(a, b), own_lanes]
        send(ref, ref, out_sem.at[1], ag_r.at[1, group(a - da, b - db)], dev)

    def share2(a, b, k):
        ref = g2.at[block(a, b), own_lanes]
        send(ref, ref, out_sem.at[1], ag_d.at[1, k], sibling)

    three = land.at[0, 28:31]

    for d in (2, 1, 3):
        push2(0, 0, d, 0)
    for d in (2, 1, 3):
        push2(0, 0, 0, d)
    share2(0, 0, 0)

    lat_t[...] = lat_v[...].T
    lat_copy = pltpu.make_async_copy(lat_t, lat_out, in_sem.at[0])
    lat_copy.start()

    for a, b in SINGLES_A:
        arrived(g2.at[block(a, b), own_lanes], ag_r.at[1, group(a, b)])
        for d in (2, 1, 3):
            push2(a, b, 0, d)
        share2(a, b, a)

    @pl.when(layer == 0)
    def _():
        second_axis(0, False)

    arrived(sq_a.at[1:4], sq_r.at[0])
    sq = sq_a[0] + sq_a[1] + sq_a[2] + sq_a[3]
    sq_b[0] = sq
    for d in (2, 1, 3):
        send(sq_b.at[0], sq_b.at[4 - d], out_sem.at[2], sq_r.at[1], along_b(d))
    arrived(three, ag_r.at[1, 3])
    for a, b in SINGLES_B:
        share2(a, b, 4)
    arrived(sq_b.at[1:4], sq_r.at[1])
    sq = sq_b[0] + sq_b[1] + sq_b[2] + sq_b[3]
    sq_d[0] = sq
    send(sq_d.at[0], sq_d.at[1], out_sem.at[2], sq_r.at[2], sibling)
    for a in (1, 3, 2):
        arrived(three, ag_r.at[1, 3 + a])
        for b in (1, 3, 2):
            share2(a, b, 4 + a)
    arrived(sq_d.at[1], sq_r.at[2])
    sq_sib = sq_d[1]
    both = jnp.concatenate([jnp.where(first, sq, sq_sib), jnp.where(first, sq_sib, sq)], axis=1)[0:1]
    scale = lax.rsqrt(both / D + EPS)

    for copy in loads[8:11]:
        copy.wait()
    for k in range(4):
        arrived(land.at[0, 28], ag_d.at[1, k])
    for k in range(4, 8):
        arrived(three, ag_d.at[1, k])

    gate = scale * lax.dot_general(wg_v[...], g2[...], NN, preferred_element_type=F32)
    up = scale * lax.dot_general(wu_v[...], g2[...], NN, preferred_element_type=F32)
    hidden = (jax.nn.gelu(gate, approximate=True) * up).astype(BF16)
    for k in range(6):
        cols = slice(384 * k, 384 * (k + 1))
        prod[2, cols, :] = lax.dot_general(wd_v[:, cols], hidden, TN, preferred_element_type=F32)
    hand_over(2, split_unit)

    @pl.when(layer == 0)
    def _():
        own = collect(0)
        z_send[...] = (keep[1, 0] - own).astype(BF16)
        send(z_send, z_recv, ms_s.at[3], ms_r.at[3], across)
        keep[1, 0] = own

    first_axis(2, split_unit)

    zero = jnp.zeros((PAD - OWN, HALF), BF16)

    for b in (2, 1, 3, 0):
        v = line_sum(2, b)
        low, high = v[0:OWN], v[OWN:CHIP]
        here = jnp.where(layer == 0, low, high)
        there = jnp.where(layer == 0, high, low)
        fin_send[b, 0:OWN, :] = there.astype(BF16)
        fin_send[b, OWN:PAD, :] = zero
        send(fin_send.at[b], fin_recv.at[(4 - b) % 4], rs_s.at[3], rs_2.at[2], across_b(b) if b else across)
        if b:
            fin_send[3 + b, 0:OWN, :] = here.astype(BF16)
            fin_send[3 + b, OWN:PAD, :] = zero
            send(fin_send.at[3 + b], fin_recv.at[7 - b], rs_s.at[3], rs_2.at[2], along_b(b))

    @pl.when(layer == 1)
    def _():
        arrived(z_recv, ms_r.at[3])
        keep[1, 0] = keep[1, 0] + z_recv[...].astype(F32)

    low, high = keep[1, 0, 0:OWN, :], keep[1, 0, OWN:CHIP, :]
    rc_send[0:OWN, :] = jnp.where(first, high, low).astype(BF16)
    rc_send[OWN:PAD, :] = zero
    sends2.append(send(rc_send, rc_recv, ms_s.at[4], ms_r.at[4], sibling))
    recon_v[:, own_lanes] = jnp.where(first, low, high).astype(BF16)
    arrived(fin_recv.at[0:7], rs_2.at[2])
    for k in range(7):
        here = here + fin_recv[k, 0:OWN, :].astype(F32)
    fin_send[7, 0:OWN, :] = here.astype(BF16)
    fin_send[7, OWN:PAD, :] = zero
    sends2.append(send(fin_send.at[7], fin_recv.at[7], ms_s.at[5], ms_r.at[5], sibling))
    out_v[:, own_lanes] = jnp.where(first, here[0:36], here[36:72]).astype(BF16)
    arrived(rc_recv, ms_r.at[4])
    recon_v[:, sib_lanes] = rc_recv[0:OWN, :]
    recon_copy = pltpu.make_async_copy(recon_v, recon_out, in_sem.at[1])
    recon_copy.start()
    arrived(fin_recv.at[7], ms_r.at[5])
    sib_half = fin_recv[7, 0:OWN, :].astype(F32)
    out_v[:, sib_lanes] = jnp.where(first, sib_half[0:36], sib_half[36:72]).astype(BF16)
    out_copy = pltpu.make_async_copy(out_v, mlp_out, in_sem.at[2])
    out_copy.start()
    all_sent(lb.at[0:31], out_sem.at[0])
    all_sent(land.at[0, 0:31], out_sem.at[1])
    all_sent(sq_all, out_sem.at[2])
    all_sent(land.at[1, 0:35], rs_s.at[1])
    all_sent(land.at[2, 0:28], rs_s.at[2])
    all_sent(fin_send.at[0:7], rs_s.at[3])

    @pl.when(layer == 0)
    def _():
        all_sent(land.at[0, 0:31], rs_s.at[0])
        all_sent(z_send, ms_s.at[3])

    settle(sends)
    settle(sends2)
    lat_copy.wait()
    recon_copy.wait()
    out_copy.wait()


def write_out(lat, recon, out, lat_out, recon_out, mlp_out):
    lat_out[...] = lat[...]
    recon_out[...] = recon[...]
    mlp_out[...] = out[...]


def per_device(
    resid_in, clt_gain, enc_w, enc_b, dec_same, dec_next, frozen_sum, mlp_gain, w_gate, w_up, w_down
):
    anywhere = pl.BlockSpec(memory_space=pl.ANY)
    dma = pltpu.SemaphoreType.DMA
    vm = pltpu.VMEM
    lat, recon, out = pl.pallas_call(
        kernel,
        out_shape=(
            jax.ShapeDtypeStruct((TOK, LAT), BF16),
            jax.ShapeDtypeStruct((OWN, TOK), BF16),
            jax.ShapeDtypeStruct((36, TOK), BF16),
        ),
        in_specs=[anywhere] * 11,
        out_specs=[anywhere] * 3,
        scratch_shapes=[
            vm((OWN, TOK), BF16), vm((1, D), F32), vm((1, LAT), F32), vm((OWN, TOK), BF16), vm((1, OWN), F32),
            vm((D, LAT), BF16), vm((LAT, D), BF16), vm((LAT, D), BF16),
            vm((CHIP, D), BF16), vm((CHIP, D), BF16), vm((CHIP, D), BF16),
            vm((D, HALF), F32), vm((LAT, HALF), F32), vm((32, PAD, TOK), BF16), vm((D, TOK), BF16),
            vm((LAT, TOK), BF16), vm((TOK, LAT), BF16),
            vm((PAD, HALF), BF16), vm((PAD, HALF), BF16), vm((OWN, HALF), F32), vm((OWN, HALF), F32),
            vm((3, D, TOK), F32), vm((3, 16, CHIP, HALF), BF16), vm((3, 35, CHIP, HALF), BF16),
            vm((3, 4, CHIP, HALF), F32), vm((3, 16, CHIP, HALF), BF16), vm((3, 4, CHIP, HALF), BF16),
            vm((CHIP, HALF), BF16), vm((CHIP, HALF), BF16), vm((PAD, HALF), BF16), vm((PAD, HALF), BF16),
            vm((OWN, TOK), BF16),
            vm((7, 8, HALF), F32), vm((4, 8, HALF), F32), vm((4, 8, HALF), F32), vm((2, 8, HALF), F32), vm((D, TOK), BF16),
            vm((8, PAD, HALF), BF16), vm((8, PAD, HALF), BF16), vm((36, TOK), BF16),
            dma((11,)), dma((3,)), dma((2, 7)), dma((2, 8)),
            dma((4,)), dma((3, 4)), dma((3, 4)), dma((3,)), dma((1,)), dma((3,)), dma((6,)), dma((6,)),
        ],
        compiler_params=pltpu.CompilerParams(
            collective_id=0, has_side_effects=True, vmem_limit_bytes=58 * 2**20
        ),
        cost_estimate=pl.CostEstimate(flops=2 * 10**9, bytes_accessed=10**7, transcendentals=0),
        name="clt_mlp",
    )(
        resid_in[0].T, clt_gain, enc_b, frozen_sum.T, mlp_gain[None],
        enc_w[0], dec_same[0], dec_next, w_gate.T, w_up.T, w_down,
    )
    lat, recon, out = pl.pallas_call(
        write_out,
        out_shape=(
            jax.ShapeDtypeStruct((TOK, LAT), BF16),
            jax.ShapeDtypeStruct((OWN, TOK), BF16),
            jax.ShapeDtypeStruct((36, TOK), BF16),
        ),
        in_specs=[pl.BlockSpec(memory_space=pltpu.VMEM)] * 3,
        out_specs=[pl.BlockSpec(memory_space=pltpu.VMEM)] * 3,
        name="write_out",
    )(lat, recon, out)
    return (lat[None], recon.T[None], out.T)


def solution(mesh):
    in_specs = (
        P("layer", "token", "latent"),
        P("layer", None),
        P("layer", None, "latent"),
        P("layer", "latent"),
        P("layer", "latent", None),
        P("latent", None),
        P("token", "latent"),
        P("latent"),
        P(None, ("layer", "latent")),
        P(None, ("layer", "latent")),
        P(("layer", "latent"), None),
    )
    out_specs = (
        P("layer", "token", "latent"),
        P("layer", "token", "latent"),
        P("token", ("layer", "latent")),
    )
    return jax.shard_map(
        per_device, mesh=mesh, in_specs=in_specs, out_specs=out_specs, check_vma=False
    )
```
